128 devices in a mesh: gr: 16 (over y, x_lo, core), gc: 8 (over x_hi, z).
Axes of the slice: x: 4 (x_hi: 2, x_lo: 2; x = x_hi * 2 + x_lo), y: 4, z: 4, core: 2. Of those that a mesh axis runs over, the one named last changes fastest.
Arguments:
- features: bfloat16 [131072, 256], P(('gr', 'gc')), may hold values from -6 to 6
- weight: bfloat16 [256, 256], replicated, may hold values from -0.375 to 0.375
- cotangent: bfloat16 [131072, 256], P(('gr', 'gc')), may hold values from -6 to 6
- blocks: bfloat16 [16, 8, 128, 128, 128], P('gr', 'gc'), may hold values from -0.21875 to 0.21875
- block_row: int32 [16, 8, 128], P('gr', 'gc'), may hold values from 0 to 63, as said below
- block_col: int32 [16, 8, 128], P('gr', 'gc'), may hold values from 0 to 127, as said below
- counts: int32 [16, 8], P('gr', 'gc'), may hold values from 16 to 128, as said below
Outputs:
- activations: bfloat16 [131072, 256], P(('gr', 'gc'))
- weight_grad: float32 [256, 256], replicated
- feature_grad: bfloat16 [131072, 256], P(('gr', 'gc'))
The draws below stay inside these ranges and needn't reach their ends.
Inputs may be any that keep to these rules, and one draw needn't show every extreme that they name: `block_row`: within one grid cell the 128 slots name distinct pairs of tile row and tile column. `block_col`: within one grid cell the 128 slots name distinct pairs of tile row and tile column. `counts`: some grid cell fills all 128 slots in every draw.
All inputs are finite; a program needn't handle non-finite values.
Results may differ from the reference program's by a relative error of at most 0.024.
Values may be sent and summed in bfloat16 or wider, within the bound.
No kernel may reach another device: no remote copies, remote signals or barrier semaphores. Data moves between devices by JAX's collectives and lax.ppermute only.
A program may use at most 192 MiB of HBM per device.

```python
import jax
import jax.numpy as jnp
from jax import lax

FEAT = 256
TILE = 128
ROWS_DEV = 1024
CAP = 128
ROW_TILES = 64
COL_TILES = 128
NODES = 131072
N_GR = 16
N_GC = 8


def tile_cells(key):
    device_keys = jax.random.split(key, N_GR * N_GC)
    picks = jax.vmap(lambda one_key: jax.random.permutation(one_key, ROW_TILES * COL_TILES)[:CAP])(device_keys)
    return picks.reshape(N_GR, N_GC, CAP).astype(jnp.int32)


def draw_block_row(key, part):
    cells = tile_cells(key)
    return (cells // COL_TILES).astype(jnp.int32)


def draw_block_col(key, part):
    cells = tile_cells(key)
    return (cells % COL_TILES).astype(jnp.int32)


def draw_counts(key, part):
    key = jax.random.fold_in(key, 7)
    first_key, second_key, third_key = jax.random.split(key, 3)
    lowest = CAP // 8
    spread = CAP - lowest + 1
    first_draw = jax.random.randint(first_key, (N_GR * N_GC,), 0, spread)
    second_draw = jax.random.randint(second_key, (N_GR * N_GC,), 0, spread)
    loads = lowest + first_draw * second_draw // spread
    busiest = jax.random.randint(third_key, (), 0, N_GR * N_GC)
    loads = jnp.where(jnp.arange(N_GR * N_GC) == busiest, CAP, loads)
    return loads.reshape(N_GR, N_GC).astype(jnp.int32)


def shard_levels(key, shape, pieces, least, largest):
    loudness, own = 1.0, jax.random.fold_in(key, 6)
    for axis_at, blocks in pieces:
        draws = jnp.exp(jax.random.uniform(jax.random.fold_in(own, axis_at), (blocks,), jnp.float32, least / len(pieces), largest / len(pieces)))
        loudness = loudness * jnp.repeat(draws, shape[axis_at] // blocks).reshape([-1 if axis == axis_at else 1 for axis in range(len(shape))])
    return loudness


def centred(key, dims, width, bound, pieces=(), held_as=jnp.bfloat16):
    array = jax.random.normal(key, dims, jnp.float32) * width
    if len(pieces) > 0:
        array = shard_levels(key, dims, pieces, -0.22, 0.18) * array
    return jnp.clip(array, min=-bound, max=bound).astype(held_as)


def setup_inputs(seed: int = 0) -> dict:
    key_list = jax.random.split(jax.random.key(seed), 8)
    features = centred(key_list[0], (NODES, FEAT), 1.0, 6.0, ((0, 128),))
    weight = centred(key_list[1], (FEAT, FEAT), FEAT ** -0.5, 0.375)
    cotangent = centred(key_list[2], (NODES, FEAT), 1.0, 6.0, ((0, 128),))
    blocks = centred(key_list[3], (N_GR, N_GC, CAP, TILE, TILE), (TILE * TILE * CAP // (3 * ROWS_DEV)) ** -0.5, 0.21875, ((0, 16), (1, 8)))
    block_row = draw_block_row(jax.random.fold_in(key_list[7], 71), 0)
    block_col = draw_block_col(jax.random.fold_in(key_list[7], 71), 0)
    counts = draw_counts(jax.random.fold_in(key_list[7], 71), 0)
    return {"features": features, "weight": weight, "cotangent": cotangent, "blocks": blocks, "block_row": block_row, "block_col": block_col, "counts": counts}


def tile_products(tile_stack, row_ids, col_ids, live_count, source_blocks, out_tiles, adjoint):
    live_mask = (jnp.arange(tile_stack.shape[0]) < live_count).astype(jnp.float32)
    wide_tiles = tile_stack.astype(jnp.float32)
    if adjoint:
        picked = source_blocks[row_ids].astype(jnp.float32)
        product = jnp.einsum('sij,sif->sjf', wide_tiles, picked)
        target_ids = col_ids
    else:
        picked = source_blocks[col_ids].astype(jnp.float32)
        product = jnp.einsum('sij,sjf->sif', wide_tiles, picked)
        target_ids = row_ids
    product = product * live_mask[:, None, None]
    return jnp.zeros((out_tiles, TILE, FEAT), jnp.float32).at[target_ids].add(product)

def rounded_add(running, cell_part):
    narrow = lax.optimization_barrier(cell_part.astype(jnp.bfloat16))
    return running + narrow.astype(jnp.float32)

def reference(features, weight, cotangent, blocks, block_row, block_col, counts):
    grid_feats = features.reshape(N_GR, N_GC, ROWS_DEV, FEAT)

    def row_part(row_index):

        def add_column(running, col_index):
            source_blocks = grid_feats[:, col_index].reshape(COL_TILES, TILE, FEAT)
            cell_part = tile_products(blocks[row_index, col_index], block_row[row_index, col_index], block_col[row_index, col_index], counts[row_index, col_index], source_blocks, ROW_TILES, False)
            return (rounded_add(running, cell_part), None)
        running, unused = lax.scan(add_column, jnp.zeros((ROW_TILES, TILE, FEAT), jnp.float32), jnp.arange(N_GC))
        return running.astype(jnp.bfloat16).reshape(ROW_TILES * TILE, FEAT)
    aggregated = lax.map(row_part, jnp.arange(N_GR)).reshape(NODES, FEAT)
    pre_act = jnp.dot(aggregated, weight, preferred_element_type=jnp.float32)
    sigmoid_val = jax.nn.sigmoid(pre_act)
    activations = (pre_act * sigmoid_val).astype(jnp.bfloat16)
    slope = sigmoid_val * (1.0 + pre_act * (1.0 - sigmoid_val))
    grad_pre = (cotangent.astype(jnp.float32) * slope).astype(jnp.bfloat16)
    weight_grad = jnp.dot(aggregated.T, grad_pre, preferred_element_type=jnp.float32) * (1.0 / jnp.sqrt(jnp.float32(NODES)))
    grad_mixed = jnp.dot(grad_pre, weight.T, preferred_element_type=jnp.float32).astype(jnp.bfloat16)
    grid_grads = grad_mixed.reshape(N_GR, ROW_TILES, TILE, FEAT)

    def column_part(col_index):

        def add_row(running, row_index):
            cell_part = tile_products(blocks[row_index, col_index], block_row[row_index, col_index], block_col[row_index, col_index], counts[row_index, col_index], grid_grads[row_index], COL_TILES, True)
            return (rounded_add(running, cell_part), None)
        running, unused = lax.scan(add_row, jnp.zeros((COL_TILES, TILE, FEAT), jnp.float32), jnp.arange(N_GR))
        return running.astype(jnp.bfloat16).reshape(N_GR, ROWS_DEV, FEAT)
    column_grads = lax.map(column_part, jnp.arange(N_GC))
    feature_grad = jnp.transpose(column_grads, (1, 0, 2, 3)).reshape(NODES, FEAT)
    return (activations, weight_grad, feature_grad)
```

```python
import functools
import math

import jax
import jax.numpy as jnp
from jax import lax
from jax.experimental import pallas as pl
from jax.experimental.pallas import tpu as pltpu
from jax.sharding import PartitionSpec as P

AXES = ("gr", "gc")
TILE = 128
CUTS = ((0, 5), (5, 11), (11, 16))
EXTRA = 2
GROUP = 8
LOAD = 8
PASS_VMEM = 40
F32 = jnp.float32
BF16 = jnp.bfloat16


def split_place(index):
    row, col = divmod(index, 8)
    y, rest = divmod(row, 4)
    xl, core = divmod(rest, 2)
    xh, z = divmod(col, 4)
    return y, xl, core, xh, z


def join_place(y, xl, core, xh, z):
    return ((y % 4) * 4 + (xl % 2) * 2 + core % 2) * 8 + (xh % 2) * 4 + z % 4


def move(value, y=0, xl=0, core=0, xh=0, z=0):
    masks = (y, xl, core, xh, z)
    pairs = []
    for index in range(128):
        at = split_place(index)
        pairs.append((index, join_place(*(a ^ b for a, b in zip(at, masks)))))
    return lax.ppermute(value, AXES, pairs)


def link_orders(ring, pair):
    near, far, other = (1, 0), (3, 0), (0, 1)
    orders = ((other, near, far), (near, far, other), (far, other, near))
    return [[({ring: r, pair: p}, r * 2 + p) for r, p in order] for order in orders]


def places(order):
    marks = [mark for _, mark in order]
    return [
        (marks[0] if p & 1 else 0) ^ (marks[1] if p & 2 else 0) ^ (marks[2] if p & 4 else 0)
        for p in range(8)
    ]


GR_LINKS = link_orders("y", "xl")
GC_LINKS = link_orders("z", "xh")


def after(value, *earlier):
    return lax.optimization_barrier((value,) + earlier)[0]


def spread(thirds, links, side=None, extra=0):
    held = [[third] for third in thirds]
    if extra:
        held[0], extra_sum = [thirds[0][:-extra]], thirds[0][-extra:]
    for step in range(3):
        sent = [parts[0] if len(parts) == 1 else jnp.concatenate(parts) for parts in held]
        if extra:
            sent[0] = jnp.concatenate(held[0] + [extra_sum]) if step else thirds[0]
        if side is not None:
            side(step, sent)
        got = [move(value, **order[step][0]) for value, order in zip(sent, links)]
        held = [parts + [value] for parts, value in zip(held, got)]
        if extra:
            held[0][-1] = got[0][:-extra]
            extra_sum = add_all(extra_sum, got[0][-extra:])
    return [array for pair in zip(sent, got) for array in pair]


def add_all(*terms):
    total = terms[0].astype(F32)
    for term in terms[1:]:
        total = total + term.astype(F32)
    return total.astype(BF16)


def collect(parts, links, extra=0):
    held = [[part] for part in parts[0::2]]
    sent = list(parts[1::2])
    extra_sum = sent[0][-extra:]
    for step in range(3):
        got = [move(value, **order[2 - step][0]) for value, order in zip(sent, links)]
        if extra:
            extra_sum = add_all(extra_sum, got[0][-extra:])
            got[0] = got[0][:-extra]
        held = [terms + [value] for terms, value in zip(held, got)]
        if step < 2:
            half = [terms[0].shape[0] // 2 for terms in held]
            sent = [add_all(*[t[h:] for t in terms]) for terms, h in zip(held, half)]
            held = [[t[:h] for t in terms] for terms, h in zip(held, half)]
            if extra:
                sent[0] = jnp.concatenate([sent[0], extra_sum])
    total = jnp.concatenate([add_all(*terms) for terms in held])
    return (total, extra_sum) if extra else total


def vmem_spec():
    return pl.BlockSpec(memory_space=pltpu.VMEM)


def smem_spec():
    return pl.BlockSpec(memory_space=pltpu.SMEM)


def any_spec():
    return pl.BlockSpec(memory_space=pl.ANY)


def hbm_spec():
    return pl.BlockSpec(memory_space=pltpu.HBM)


def cost(flops, moved):
    return pl.CostEstimate(flops=flops, bytes_accessed=moved, transcendentals=0)


def third_shapes(pieces=1, extra=0):
    counts = [pieces * (hi - lo) for lo, hi in CUTS]
    counts[0] += extra
    return [jax.ShapeDtypeStruct((count, TILE, TILE), BF16) for count in counts]


def third_of(tile):
    return next((at, tile - lo) for at, (lo, hi) in enumerate(CUTS) if lo <= tile < hi)


def turn_kernel(core_ref, own_ref, sib_ref, *out_refs):
    lanes = pl.ds(pl.multiple_of(core_ref[0] * TILE, TILE), TILE)
    for half, ref in enumerate((own_ref, sib_ref)):
        for tile in range(8):
            third, at = third_of(half * 8 + tile)
            out_refs[third][at] = ref[tile * TILE : (tile + 1) * TILE, lanes].T


def turn_in(core, own, sib):
    return pl.pallas_call(
        turn_kernel,
        out_shape=third_shapes(),
        in_specs=[smem_spec(), vmem_spec(), vmem_spec()],
        out_specs=[vmem_spec()] * 3,
        compiler_params=pltpu.CompilerParams(vmem_limit_bytes=8 << 20),
        cost_estimate=cost(0, 2 << 20),
        name="turn_in",
    )(core, own, sib)


def third_rows(links):
    rows = [[] for _ in range(6)]
    for third, (order, (lo, hi)) in enumerate(zip(links, CUTS)):
        for p, mark in enumerate(places(order)):
            rows[2 * third + p // 4].append(((p % 4) * (hi - lo), mark * 16 + lo, hi - lo))
    return rows


def array_place(ids):
    mark, tile = ids // 16, ids % 16
    turn, other = mark // 2, mark % 2
    near = ((turn == 1) | (turn == 2)).astype(jnp.int32)
    far = (turn >= 2).astype(jnp.int32)
    bits = ((other, near, far), (near, far, other), (far, other, near))
    array, row = jnp.zeros_like(ids), jnp.zeros_like(ids)
    for third, ((lo, hi), (a, b, c)) in enumerate(zip(CUTS, bits)):
        here = (tile >= lo) & (tile < hi)
        array = jnp.where(here, 2 * third + c, array)
        row = jnp.where(here, (a + 2 * b) * (hi - lo) + tile - lo, row)
    return array, row


def order_slots(array, row, target, dead):
    key = jnp.where(dead, 6, array).reshape(-1)
    count = key.shape[0]
    at = jnp.arange(count, dtype=jnp.int32)
    packed = (row + 32 * target).reshape(-1) + 4096 * at
    ahead = (key[None, :] < key[:, None]) | (
        (key[None, :] == key[:, None]) & (at[None, :] < at[:, None])
    )
    rank = jnp.sum(ahead.astype(jnp.int32), axis=1)
    listed = jnp.sum(jnp.where(rank[None, :] == at[:, None], packed[None, :], 0), axis=1)
    bounds = jnp.sum((key[None, :] < jnp.arange(7, dtype=jnp.int32)[:, None]).astype(jnp.int32), axis=1)
    return listed, bounds


def pass_kernel(adjoint, live_ref, list_ref, bound_ref, own_tiles, sib_tiles, *rest):
    sources, targets = rest[:6], rest[6:12]
    tile_buf, total, tile_sems = rest[12:]
    slots = own_tiles.shape[0]
    lists = (own_tiles, sib_tiles)
    groups = [lax.div(live_ref[side] + (LOAD - 1), LOAD) for side in range(2)]

    def tile_copy(side, group):
        first = pl.multiple_of(group * LOAD, LOAD)
        return pltpu.make_async_copy(
            lists[side].at[pl.ds(first, LOAD)],
            tile_buf.at[pl.ds(side * slots + first, LOAD)],
            tile_sems.at[side, group],
        )

    for side in range(2):
        pl.loop(0, groups[side])(lambda group, side=side: tile_copy(side, group).start())

    @pl.loop(0, total.shape[0] // 3)
    def _(at):
        total[pl.ds(at * 3, 3)] = jnp.zeros((3,) + total.shape[1:], F32)

    for side in range(2):
        pl.loop(0, groups[side])(lambda group, side=side: tile_copy(side, group).wait())

    dims = (((1,), (0,)), ((), ())) if adjoint else (((1,), (1,)), ((), ()))
    for array, source in enumerate(sources):
        first, last = bound_ref[array], bound_ref[array + 1]

        @pl.loop(0, lax.div(last - first + (GROUP - 1), GROUP))
        def _(group, source=source, first=first, last=last):
            products, places_to = [], []
            for step in range(GROUP):
                at = first + group * GROUP + step
                live = at < last
                entry = jnp.where(live, list_ref[jnp.minimum(at, 2 * slots - 1)], 0)
                places_to.append(jnp.where(live, (entry >> 5) & 127, 128))
                products.append(
                    lax.dot_general(
                        source[entry & 31],
                        tile_buf[entry >> 12],
                        dims,
                        preferred_element_type=F32,
                    )
                )
            for to, product in zip(places_to, products):
                total[to] = total[to] + product

    if adjoint:
        first, last = sources[0].shape[0] - EXTRA, sources[0].shape[0]
        extra = sources[0][first:last].astype(F32) + sources[1][first:last].astype(F32)
        targets[1][first:last] = extra.astype(BF16)
    for target, rows in zip(targets, third_rows(GR_LINKS if adjoint else GC_LINKS)):
        for first, at, count in rows:
            for step in range(count):
                target[first + step] = total[at + step].astype(BF16)


def block_pass(adjoint, live, listed, bounds, own_tiles, sib_tiles, sources):
    slots = own_tiles.shape[0]
    out_shape = [shape for shape in third_shapes(4) for _ in range(2)]
    if adjoint:
        out_shape[1] = third_shapes(4, EXTRA)[0]
    return pl.pallas_call(
        functools.partial(pass_kernel, adjoint),
        out_shape=out_shape,
        in_specs=[smem_spec()] * 3 + [any_spec()] * 2 + [vmem_spec()] * 6,
        out_specs=[vmem_spec()] * 6,
        scratch_shapes=[
            pltpu.VMEM((2 * slots, TILE, TILE), BF16),
            pltpu.VMEM((129, TILE, TILE), F32),
            pltpu.SemaphoreType.DMA((2, slots // LOAD)),
        ],
        compiler_params=pltpu.CompilerParams(vmem_limit_bytes=PASS_VMEM << 20),
        cost_estimate=cost(2 * 256 * TILE * TILE * TILE, 24 << 20),
        name="block_adjoint" if adjoint else "block_pass",
    )(live, listed, bounds, own_tiles, sib_tiles, *sources)


def dense_kernel(core_ref, weight_ref, own_cot, sib_cot, own_sums, sib_sums, *rest):
    act_ref, *mixed_refs, mixed_buf, wgrad_ref = rest
    core = core_ref[0]
    own_weight = weight_ref[pl.ds(pl.multiple_of(core * TILE, TILE), TILE), :]
    sib_weight = weight_ref[pl.ds(pl.multiple_of((1 - core) * TILE, TILE), TILE), :]
    wgrad_ref[...] = jnp.zeros(wgrad_ref.shape, F32)
    for half, cot_ref in enumerate((own_cot, sib_cot)):

        @pl.loop(0, 4)
        def _(pair, half=half, cot_ref=cot_ref):
            for step in range(2):
                tile = pair * 2 + step
                rows = pl.ds(pl.multiple_of(tile * TILE, TILE), TILE)
                own = own_sums[half * 8 + tile]
                sib = sib_sums[(1 - half) * 8 + tile]
                pre = jnp.dot(own.T, own_weight, preferred_element_type=F32)
                pre = pre + jnp.dot(sib.T, sib_weight, preferred_element_type=F32)
                sigmoid = jax.nn.sigmoid(pre)
                if half == 0:
                    act_ref[rows, :] = (pre * sigmoid).astype(BF16)
                slope = sigmoid * (1.0 + pre * (1.0 - sigmoid))
                grad = (cot_ref[rows, :].astype(F32) * slope).astype(BF16)
                wgrad_ref[...] += jnp.dot(own, grad, preferred_element_type=F32)
                mixed_buf[half * 8 + tile] = lax.dot_general(
                    own_weight, grad, (((1,), (1,)), ((), ())), preferred_element_type=F32
                ).astype(BF16)

    for ref, (lo, hi) in zip(mixed_refs, CUTS):
        ref[: hi - lo] = mixed_buf[lo:hi]
    for part in range(EXTRA):
        extra = wgrad_ref[:, part * TILE : (part + 1) * TILE]
        mixed_refs[0][CUTS[0][1] + part] = extra.astype(BF16)


def dense(core, weight, own_cot, sib_cot, own_sums, sib_sums):
    outs = pl.pallas_call(
        dense_kernel,
        out_shape=[
            jax.ShapeDtypeStruct(own_cot.shape, BF16),
        ]
        + third_shapes(1, EXTRA),
        in_specs=[smem_spec()] + [vmem_spec()] * 5,
        out_specs=[vmem_spec()] * 4,
        scratch_shapes=[
            pltpu.VMEM((16, TILE, TILE), BF16),
            pltpu.VMEM((TILE, EXTRA * TILE), F32),
        ],
        compiler_params=pltpu.CompilerParams(vmem_limit_bytes=24 << 20),
        cost_estimate=cost(2 * 2048 * 256 * 512, 4 << 20),
        name="dense",
    )(core, weight, own_cot, sib_cot, own_sums, sib_sums)
    return outs[0], outs[1:]


def back_kernel(core_ref, own_ref, sib_ref, out_ref):
    core = core_ref[0]
    for ref, half in ((own_ref, core), (sib_ref, 1 - core)):
        lanes = pl.ds(pl.multiple_of(half * TILE, TILE), TILE)
        for tile in range(8):
            out_ref[tile * TILE : (tile + 1) * TILE, lanes] = ref[tile].T


def turn_back(core, own_part, sib_part):
    return pl.pallas_call(
        back_kernel,
        out_shape=jax.ShapeDtypeStruct((8 * TILE, 2 * TILE), BF16),
        in_specs=[smem_spec()] + [vmem_spec()] * 2,
        out_specs=vmem_spec(),
        compiler_params=pltpu.CompilerParams(vmem_limit_bytes=8 << 20),
        cost_estimate=cost(0, 1 << 20),
        name="turn_back",
    )(core, own_part, sib_part)


def body(features, weight, cotangent, blocks, block_row, block_col, counts):
    row_at, col_at = lax.axis_index("gr"), lax.axis_index("gc")
    y, xl, core = row_at // 4, (row_at // 2) % 2, row_at % 2
    xh, z = col_at // 4, col_at % 4
    core_arg = core.reshape(1).astype(jnp.int32)

    sib_feats = move(features, core=1)
    slices = turn_in(core_arg, features, sib_feats)

    own_tiles = blocks[0, 0]
    slots = own_tiles.shape[0]
    fetched = []

    def fetch(step, sent):
        if step == 1:
            sent = sent[:1]
            live = jnp.broadcast_to(after(counts[0, 0], *sent), (slots,))
            rows, cols = after(block_row[0, 0], *sent), after(block_col[0, 0], *sent)
            lists = jnp.stack([rows, cols, live])
            fetched.extend([lists, move(lists, core=1)])
        if step == 2:
            fetched.append(move(after(cotangent, *sent), core=1))

    gathered = spread(slices, GR_LINKS, fetch)
    own_lists, sib_lists, sib_cot = fetched
    sib_tiles = move(after(own_tiles, slices[0]), core=1)
    lists = jnp.stack([own_lists, sib_lists], axis=1)
    rows, cols, live = lists[0], lists[1], lists[2, :, 0]
    side = jnp.arange(2, dtype=jnp.int32)[:, None]
    part = rows // 8
    row_ids = (((part % 4) ^ z) * 2 + ((part // 4) ^ xh)) * 16 + side * 8 + rows % 8
    part = cols // 8
    col_ids = ((part // 4) ^ y) * 32 + (((part // 2) % 2) ^ xl) * 16
    col_ids = col_ids + ((part % 2) ^ core) * 8 + cols % 8
    dead = jnp.arange(slots, dtype=jnp.int32)[None, :] >= live[:, None]
    by_col = order_slots(*array_place(col_ids), row_ids, dead)
    by_col = (after(by_col[0], sib_cot), by_col[1])
    by_row = order_slots(*array_place(row_ids), col_ids, dead)

    parts = block_pass(False, live, *by_col, own_tiles, sib_tiles, gathered)
    own_sums = collect(parts, GC_LINKS)
    sib_sums = move(own_sums, core=1)

    activations, mixed = dense(core_arg, weight, cotangent, sib_cot, own_sums, sib_sums)

    gathered = spread(mixed, GC_LINKS, extra=EXTRA)
    parts = block_pass(True, live, *by_row, own_tiles, sib_tiles, gathered)
    grads, wgrad = collect(parts, GR_LINKS, EXTRA)
    last = move(jnp.concatenate([grads[8:], wgrad]), core=1)
    feature_grad = turn_back(core_arg, grads[:8], last)

    node_total = features.shape[0] * lax.axis_size("gr") * lax.axis_size("gc")
    halves = [jnp.concatenate([part[-2], part[-1]], axis=1).astype(F32) for part in (wgrad, last)]
    weight_grad = jnp.where(core == 0, jnp.concatenate(halves), jnp.concatenate(halves[::-1]))
    weight_grad = weight_grad * (1.0 / math.sqrt(node_total))
    return (activations, weight_grad, feature_grad)


def solution(mesh):
    return jax.shard_map(
        body,
        mesh=mesh,
        in_specs=(
            P(("gr", "gc"), None),
            P(),
            P(("gr", "gc"), None),
            P("gr", "gc", None, None, None),
            P("gr", "gc", None),
            P("gr", "gc", None),
            P("gr", "gc"),
        ),
        out_specs=(P(("gr", "gc"), None), P(), P(("gr", "gc"), None)),
        check_vma=False,
    )
```

```python
import functools
import math

import jax
import jax.numpy as jnp
from jax import lax
from jax.experimental import pallas as pl
from jax.experimental.pallas import tpu as pltpu
from jax.sharding import PartitionSpec as P

AXES = ("gr", "gc")
TILE = 128
CUTS = ((0, 6), (6, 11), (11, 16))
SIDE = 1
EXTRA = 2
GROUP = 8
LOAD = 8
PASS_VMEM = 26
F32 = jnp.float32
BF16 = jnp.bfloat16


def split_place(index):
    row, col = divmod(index, 8)
    y, rest = divmod(row, 4)
    xl, core = divmod(rest, 2)
    xh, z = divmod(col, 4)
    return y, xl, core, xh, z


def join_place(y, xl, core, xh, z):
    return ((y % 4) * 4 + (xl % 2) * 2 + core % 2) * 8 + (xh % 2) * 4 + z % 4


def move(value, y=0, xl=0, core=0, xh=0, z=0):
    masks = (y, xl, core, xh, z)
    pairs = []
    for index in range(128):
        at = split_place(index)
        pairs.append((index, join_place(*(a ^ b for a, b in zip(at, masks)))))
    return lax.ppermute(value, AXES, pairs)


def link_orders(ring, pair):
    near, far, other = (1, 0), (3, 0), (0, 1)
    orders = ((other, near, far), (near, far, other), (far, other, near))
    return [[({ring: r, pair: p}, r * 2 + p) for r, p in order] for order in orders]


def places(order):
    marks = [mark for _, mark in order]
    return [
        (marks[0] if p & 1 else 0) ^ (marks[1] if p & 2 else 0) ^ (marks[2] if p & 4 else 0)
        for p in range(8)
    ]


GR_LINKS = link_orders("y", "xl")
GC_LINKS = link_orders("z", "xh")


def after(value, *earlier):
    return lax.optimization_barrier((value,) + earlier)[0]


def spread(thirds, links, hook=None, extra=0):
    held = [[third] for third in thirds]
    if extra:
        held[SIDE], extra_sum = [thirds[SIDE][:-extra]], thirds[SIDE][-extra:]
    for step in range(3):
        sent = [parts[0] if len(parts) == 1 else jnp.concatenate(parts) for parts in held]
        if extra:
            sent[SIDE] = jnp.concatenate(held[SIDE] + [extra_sum]) if step else thirds[SIDE]
        if hook is not None:
            hook(step, sent)
        got = [move(value, **order[step][0]) for value, order in zip(sent, links)]
        held = [parts + [value] for parts, value in zip(held, got)]
        if extra:
            held[SIDE][-1] = got[SIDE][:-extra]
            extra_sum = add_all(extra_sum, got[SIDE][-extra:])
    return [array for pair in zip(sent, got) for array in pair]


def add_all(*terms):
    total = terms[0].astype(F32)
    for term in terms[1:]:
        total = total + term.astype(F32)
    return total.astype(BF16)


def collect(parts, links, extra=0):
    held = [[part] for part in parts[0::2]]
    sent = list(parts[1::2])
    extra_sum = sent[SIDE][-extra:]
    for step in range(3):
        got = [move(value, **order[2 - step][0]) for value, order in zip(sent, links)]
        added = list(got)
        if extra:
            extra_sum = add_all(extra_sum, got[SIDE][-extra:])
            added[SIDE] = got[SIDE][:-extra]
        held = [terms + [value] for terms, value in zip(held, added)]
        if step < 2:
            half = [terms[0].shape[0] // 2 for terms in held]
            sent = [add_all(*[t[h:] for t in terms]) for terms, h in zip(held, half)]
            held = [[t[:h] for t in terms] for terms, h in zip(held, half)]
            if extra:
                sent[SIDE] = jnp.concatenate([sent[SIDE], extra_sum])
    total = jnp.concatenate([add_all(*terms) for terms in held])
    return (total, extra_sum) if extra else total


def vmem_spec():
    return pl.BlockSpec(memory_space=pltpu.VMEM)


def smem_spec():
    return pl.BlockSpec(memory_space=pltpu.SMEM)


def any_spec():
    return pl.BlockSpec(memory_space=pl.ANY)


def hbm_spec():
    return pl.BlockSpec(memory_space=pltpu.HBM)


def cost(flops, moved):
    return pl.CostEstimate(flops=flops, bytes_accessed=moved, transcendentals=0)


def third_shapes(pieces=1, extra=0):
    counts = [pieces * (hi - lo) for lo, hi in CUTS]
    counts[SIDE] += extra
    return [jax.ShapeDtypeStruct((count, TILE, TILE), BF16) for count in counts]


def third_of(tile):
    return next((at, tile - lo) for at, (lo, hi) in enumerate(CUTS) if lo <= tile < hi)


def turn_kernel(core_ref, own_ref, sib_ref, *out_refs):
    lanes = pl.ds(pl.multiple_of(core_ref[0] * TILE, TILE), TILE)
    for half, ref in enumerate((own_ref, sib_ref)):
        for tile in range(8):
            third, at = third_of(half * 8 + tile)
            out_refs[third][at] = ref[tile * TILE : (tile + 1) * TILE, lanes].T


def turn_in(core, own, sib):
    return pl.pallas_call(
        turn_kernel,
        out_shape=third_shapes(),
        in_specs=[smem_spec(), vmem_spec(), vmem_spec()],
        out_specs=[vmem_spec()] * 3,
        compiler_params=pltpu.CompilerParams(vmem_limit_bytes=8 << 20),
        cost_estimate=cost(0, 2 << 20),
        name="turn_in",
    )(core, own, sib)


def array_place(ids):
    mark, tile = ids // 16, ids % 16
    turn, other = mark // 2, mark % 2
    near = ((turn == 1) | (turn == 2)).astype(jnp.int32)
    far = (turn >= 2).astype(jnp.int32)
    bits = ((other, near, far), (near, far, other), (far, other, near))
    array, row = jnp.zeros_like(ids), jnp.zeros_like(ids)
    for third, ((lo, hi), (a, b, c)) in enumerate(zip(CUTS, bits)):
        here = (tile >= lo) & (tile < hi)
        array = jnp.where(here, 2 * third + c, array)
        row = jnp.where(here, (a + 2 * b) * (hi - lo) + tile - lo, row)
    return array, row


def total_row(ids):
    array, row = array_place(ids)
    first = sum(jnp.where(array // 2 == third, 4 * lo, 0) for third, (lo, _) in enumerate(CUTS))
    return first + row + 64 * (1 - array % 2)


def order_slots(source_ids, target_ids, dead):
    array, row = array_place(source_ids)
    target = total_row(target_ids)
    late = jnp.where(target < 64, 3, 6)
    key = jnp.where(dead, 9, array // 2 + jnp.where(array % 2 == 1, late, 0)).reshape(-1)
    at = jnp.arange(key.shape[0], dtype=jnp.int32)
    packed = (row + 32 * target).reshape(-1) + 4096 * at
    ahead = (key[None, :] < key[:, None]) | (
        (key[None, :] == key[:, None]) & (at[None, :] < at[:, None])
    )
    rank = jnp.sum(ahead.astype(jnp.int32), axis=1)
    listed = jnp.sum(jnp.where(rank[None, :] == at[:, None], packed[None, :], 0), axis=1)
    marks = jnp.arange(10, dtype=jnp.int32)[:, None]
    bounds = jnp.sum((key[None, :] < marks).astype(jnp.int32), axis=1)
    return listed, bounds


def add_products(adjoint, first_class, list_ref, bound_ref, sources, tiles, total, base=0):
    dims = (((1,), (0,)), ((), ())) if adjoint else (((1,), (1,)), ((), ()))
    final, unused = tiles.shape[0] - 1, total.shape[0] - 1
    for index, source in enumerate(sources):
        first, last = bound_ref[first_class + index], bound_ref[first_class + index + 1]

        @pl.loop(0, lax.div(last - first + (GROUP - 1), GROUP))
        def _(group, source=source, first=first, last=last):
            products, places_to = [], []
            for step in range(GROUP):
                at = first + group * GROUP + step
                live = at < last
                entry = jnp.where(live, list_ref[jnp.minimum(at, final)], 0)
                places_to.append(jnp.where(live, ((entry >> 5) & 127) - base, unused))
                products.append(
                    lax.dot_general(
                        source[entry & 31],
                        tiles[entry >> 12],
                        dims,
                        preferred_element_type=F32,
                    )
                )
            for to, product in zip(places_to, products):
                total[to] = total[to] + product


def clear(total):
    @pl.loop(0, total.shape[0] // 3)
    def _(at):
        total[pl.ds(at * 3, 3)] = jnp.zeros((3,) + total.shape[1:], F32)


def give(total, result):
    @pl.loop(0, 32)
    def _(at):
        result[pl.ds(at * 4, 4)] = total[pl.ds(at * 4, 4)].astype(BF16)


def load_kernel(live_ref, list_ref, bound_ref, own_tiles, sib_tiles, *rest):
    sources, (result, tiles, total, sems) = rest[:3], rest[3:]
    slots = own_tiles.shape[0]
    lists = (own_tiles, sib_tiles)
    groups = [lax.div(live_ref[side] + (LOAD - 1), LOAD) for side in range(2)]

    def tile_copy(side, group):
        first = pl.multiple_of(group * LOAD, LOAD)
        return pltpu.make_async_copy(
            lists[side].at[pl.ds(first, LOAD)],
            tiles.at[pl.ds(side * slots + first, LOAD)],
            sems.at[side, group],
        )

    for side in range(2):
        pl.loop(0, groups[side])(lambda group, side=side: tile_copy(side, group).start())
    clear(total)
    for side in range(2):
        pl.loop(0, groups[side])(lambda group, side=side: tile_copy(side, group).wait())
    add_products(False, 0, list_ref, bound_ref, sources, tiles, total)
    give(total, result)


def early_kernel(list_ref, bound_ref, tiles, *rest):
    sources, (result, total) = rest[:3], rest[3:]
    clear(total)
    add_products(True, 0, list_ref, bound_ref, sources, tiles, total)
    give(total, result)


def late_kernel(adjoint, kept, list_ref, bound_ref, tiles, before, *rest):
    sources, rest = rest[:3], rest[3:]
    if adjoint and not kept:
        extra_ref, *rest = rest
        rows = extra_ref.shape[0] - EXTRA, extra_ref.shape[0]
        extra = extra_ref[rows[0] : rows[1]].astype(F32) + sources[SIDE][rows[0] : rows[1]].astype(F32)
        rest[SIDE][rows[0] : rows[1]] = extra.astype(BF16)
    *targets, total = rest
    base = 64 if kept else 0

    @pl.loop(0, 16)
    def _(at):
        total[pl.ds(at * 4, 4)] = before[pl.ds(base + at * 4, 4)].astype(F32)

    add_products(
        adjoint, 6 if kept else 3, list_ref, bound_ref, sources, tiles, total, base
    )
    for target, (lo, hi) in zip(targets, CUTS):
        for row in range(4 * (hi - lo)):
            target[row] = total[4 * lo + row].astype(BF16)


TOTAL = jax.ShapeDtypeStruct((128, TILE, TILE), BF16)
SUMS = pltpu.VMEM((129, TILE, TILE), F32)


def pass_params():
    return pltpu.CompilerParams(vmem_limit_bytes=PASS_VMEM << 20)


def early_pass(adjoint, live, listed, bounds, tiles, sources):
    estimate = cost(128 * TILE * TILE * TILE, 16 << 20)
    if adjoint:
        return tiles, pl.pallas_call(
            early_kernel,
            out_shape=TOTAL,
            in_specs=[smem_spec()] * 2 + [vmem_spec()] * 4,
            out_specs=vmem_spec(),
            scratch_shapes=[SUMS],
            compiler_params=pass_params(),
            cost_estimate=estimate,
            name="early_adjoint",
        )(listed, bounds, tiles, *sources)
    slots = tiles[0].shape[0]
    total, tiles = pl.pallas_call(
        load_kernel,
        out_shape=[TOTAL, jax.ShapeDtypeStruct((2 * slots, TILE, TILE), BF16)],
        in_specs=[smem_spec()] * 3 + [any_spec()] * 2 + [vmem_spec()] * 3,
        out_specs=[vmem_spec()] * 2,
        scratch_shapes=[SUMS, pltpu.SemaphoreType.DMA((2, slots // LOAD))],
        compiler_params=pass_params(),
        cost_estimate=estimate,
        name="early_pass",
    )(live, listed, bounds, *tiles, *sources)
    return tiles, total


def late_pass(adjoint, kept, listed, bounds, tiles, total, sources, extra=()):
    return pl.pallas_call(
        functools.partial(late_kernel, adjoint, kept),
        out_shape=third_shapes(4, EXTRA if extra else 0),
        in_specs=[smem_spec()] * 2 + [vmem_spec()] * (5 + len(extra)),
        out_specs=[vmem_spec()] * 3,
        scratch_shapes=[pltpu.VMEM((65, TILE, TILE), F32)],
        compiler_params=pass_params(),
        cost_estimate=cost(64 * TILE * TILE * TILE, 8 << 20),
        name=("kept" if kept else "sent") + ("_adjoint" if adjoint else "_pass"),
    )(listed, bounds, tiles, total, *sources, *extra)


def block_pass(adjoint, live, order, tiles, sources):
    extra = sources[2 * SIDE : 2 * SIDE + 1] if adjoint else ()
    tiles, total = early_pass(adjoint, live, *order, tiles, sources[0::2])
    sent = late_pass(adjoint, False, *order, tiles, total, sources[1::2], extra)
    held = late_pass(adjoint, True, *order, tiles, total, sources[1::2])
    return [array for pair in zip(held, sent) for array in pair], tiles


def dense_kernel(core_ref, weight_ref, own_cot, sib_cot, own_sums, sib_sums, *rest):
    act_ref, *mixed_refs, mixed_buf, wgrad_ref = rest
    core = core_ref[0]
    own_weight = weight_ref[pl.ds(pl.multiple_of(core * TILE, TILE), TILE), :]
    sib_weight = weight_ref[pl.ds(pl.multiple_of((1 - core) * TILE, TILE), TILE), :]
    wgrad_ref[...] = jnp.zeros(wgrad_ref.shape, F32)
    for half, cot_ref in enumerate((own_cot, sib_cot)):

        @pl.loop(0, 4)
        def _(pair, half=half, cot_ref=cot_ref):
            for step in range(2):
                tile = pair * 2 + step
                rows = pl.ds(pl.multiple_of(tile * TILE, TILE), TILE)
                own = own_sums[half * 8 + tile]
                sib = sib_sums[(1 - half) * 8 + tile]
                pre = jnp.dot(own.T, own_weight, preferred_element_type=F32)
                pre = pre + jnp.dot(sib.T, sib_weight, preferred_element_type=F32)
                sigmoid = jax.nn.sigmoid(pre)
                if half == 0:
                    act_ref[rows, :] = (pre * sigmoid).astype(BF16)
                slope = sigmoid * (1.0 + pre * (1.0 - sigmoid))
                grad = (cot_ref[rows, :].astype(F32) * slope).astype(BF16)
                wgrad_ref[...] += jnp.dot(own, grad, preferred_element_type=F32)
                mixed_buf[half * 8 + tile] = lax.dot_general(
                    own_weight, grad, (((1,), (1,)), ((), ())), preferred_element_type=F32
                ).astype(BF16)

    for ref, (lo, hi) in zip(mixed_refs, CUTS):
        ref[: hi - lo] = mixed_buf[lo:hi]
    for part in range(EXTRA):
        extra = wgrad_ref[:, part * TILE : (part + 1) * TILE]
        mixed_refs[SIDE][CUTS[SIDE][1] - CUTS[SIDE][0] + part] = extra.astype(BF16)


def dense(core, weight, own_cot, sib_cot, own_sums, sib_sums):
    outs = pl.pallas_call(
        dense_kernel,
        out_shape=[
            jax.ShapeDtypeStruct(own_cot.shape, BF16),
        ]
        + third_shapes(1, EXTRA),
        in_specs=[smem_spec()] + [vmem_spec()] * 5,
        out_specs=[vmem_spec()] * 4,
        scratch_shapes=[
            pltpu.VMEM((16, TILE, TILE), BF16),
            pltpu.VMEM((TILE, EXTRA * TILE), F32),
        ],
        compiler_params=pltpu.CompilerParams(vmem_limit_bytes=24 << 20),
        cost_estimate=cost(2 * 2048 * 256 * 512, 4 << 20),
        name="dense",
    )(core, weight, own_cot, sib_cot, own_sums, sib_sums)
    return outs[0], outs[1:]


def back_kernel(core_ref, own_ref, sib_ref, out_ref):
    core = core_ref[0]
    for ref, half in ((own_ref, core), (sib_ref, 1 - core)):
        lanes = pl.ds(pl.multiple_of(half * TILE, TILE), TILE)
        for tile in range(8):
            out_ref[tile * TILE : (tile + 1) * TILE, lanes] = ref[tile].T


def turn_back(core, own_part, sib_part):
    return pl.pallas_call(
        back_kernel,
        out_shape=jax.ShapeDtypeStruct((8 * TILE, 2 * TILE), BF16),
        in_specs=[smem_spec()] + [vmem_spec()] * 2,
        out_specs=vmem_spec(),
        compiler_params=pltpu.CompilerParams(vmem_limit_bytes=8 << 20),
        cost_estimate=cost(0, 1 << 20),
        name="turn_back",
    )(core, own_part, sib_part)


def body(features, weight, cotangent, blocks, block_row, block_col, counts):
    row_at, col_at = lax.axis_index("gr"), lax.axis_index("gc")
    y, xl, core = row_at // 4, (row_at // 2) % 2, row_at % 2
    xh, z = col_at // 4, col_at % 4
    core_arg = core.reshape(1).astype(jnp.int32)

    sib_feats = move(features, core=1)
    slices = turn_in(core_arg, features, sib_feats)

    own_tiles = blocks[0, 0]
    slots = own_tiles.shape[0]
    fetched = []

    def fetch(step, sent):
        if step == 2:
            event = sent[2]
            live = jnp.broadcast_to(after(counts[0, 0], event), (slots,))
            rows, cols = after(block_row[0, 0], event), after(block_col[0, 0], event)
            lists = jnp.stack([rows, cols, live])
            fetched.extend([lists, move(lists, core=1), move(after(cotangent, event), core=1)])

    gathered = spread(slices, GR_LINKS, fetch)
    own_lists, sib_lists, sib_cot = fetched
    sib_tiles = move(after(own_tiles, slices[0]), core=1)
    lists = jnp.stack([own_lists, sib_lists], axis=1)
    rows, cols, live = lists[0], lists[1], lists[2, :, 0]
    side = jnp.arange(2, dtype=jnp.int32)[:, None]
    part = rows // 8
    row_ids = (((part % 4) ^ z) * 2 + ((part // 4) ^ xh)) * 16 + side * 8 + rows % 8
    part = cols // 8
    col_ids = ((part // 4) ^ y) * 32 + (((part // 2) % 2) ^ xl) * 16
    col_ids = col_ids + ((part % 2) ^ core) * 8 + cols % 8
    dead = jnp.arange(slots, dtype=jnp.int32)[None, :] >= live[:, None]
    by_col = order_slots(col_ids, row_ids, dead)
    by_col = (after(by_col[0], sib_cot), by_col[1])
    by_row = order_slots(row_ids, col_ids, dead)

    parts, tiles = block_pass(False, live, by_col, (own_tiles, sib_tiles), gathered)
    own_sums = collect(parts, GC_LINKS)
    sib_sums = move(own_sums, core=1)

    activations, mixed = dense(core_arg, weight, cotangent, sib_cot, own_sums, sib_sums)

    gathered = spread(mixed, GC_LINKS, extra=EXTRA)
    parts, _ = block_pass(True, live, by_row, tiles, gathered)
    grads, wgrad = collect(parts, GR_LINKS, EXTRA)
    last = move(jnp.concatenate([grads[8:], wgrad]), core=1)
    feature_grad = turn_back(core_arg, grads[:8], last)

    node_total = features.shape[0] * lax.axis_size("gr") * lax.axis_size("gc")
    halves = [jnp.concatenate([part[-2], part[-1]], axis=1).astype(F32) for part in (wgrad, last)]
    weight_grad = jnp.where(core == 0, jnp.concatenate(halves), jnp.concatenate(halves[::-1]))
    weight_grad = weight_grad * (1.0 / math.sqrt(node_total))
    return (activations, weight_grad, feature_grad)


def solution(mesh):
    return jax.shard_map(
        body,
        mesh=mesh,
        in_specs=(
            P(("gr", "gc"), None),
            P(),
            P(("gr", "gc"), None),
            P("gr", "gc", None, None, None),
            P("gr", "gc", None),
            P("gr", "gc", None),
            P("gr", "gc"),
        ),
        out_specs=(P(("gr", "gc"), None), P(), P(("gr", "gc"), None)),
        check_vma=False,
    )
```

```python
import functools
import math

import jax
import jax.numpy as jnp
from jax import lax
from jax.experimental import pallas as pl
from jax.experimental.pallas import tpu as pltpu
from jax.sharding import PartitionSpec as P

AXES = ("gr", "gc")
TILE = 128
CUTS = ((0, 6), (6, 11), (11, 16))
SIDE = 1
EXTRA = 2
GROUP = 8
LOAD = 8
PASS_VMEM = 26
F32 = jnp.float32
BF16 = jnp.bfloat16


def split_place(index):
    row, col = divmod(index, 8)
    y, rest = divmod(row, 4)
    xl, core = divmod(rest, 2)
    xh, z = divmod(col, 4)
    return y, xl, core, xh, z


def join_place(y, xl, core, xh, z):
    return ((y % 4) * 4 + (xl % 2) * 2 + core % 2) * 8 + (xh % 2) * 4 + z % 4


def move(value, y=0, xl=0, core=0, xh=0, z=0):
    masks = (y, xl, core, xh, z)
    pairs = []
    for index in range(128):
        at = split_place(index)
        pairs.append((index, join_place(*(a ^ b for a, b in zip(at, masks)))))
    return lax.ppermute(value, AXES, pairs)


def link_orders(ring, pair):
    near, far, other = (1, 0), (3, 0), (0, 1)
    orders = ((near, far, other), (far, other, near), (other, near, far))
    return [[({ring: r, pair: p}, r * 2 + p) for r, p in order] for order in orders]


def places(order):
    marks = [mark for _, mark in order]
    return [
        (marks[0] if p & 1 else 0) ^ (marks[1] if p & 2 else 0) ^ (marks[2] if p & 4 else 0)
        for p in range(8)
    ]


GR_LINKS = link_orders("y", "xl")
GC_LINKS = link_orders("z", "xh")


def after(value, *earlier):
    return lax.optimization_barrier((value,) + earlier)[0]


def spread(thirds, links, hook=None, extra=0):
    held = [[third] for third in thirds]
    if extra:
        held[SIDE], extra_sum = [thirds[SIDE][:-extra]], thirds[SIDE][-extra:]
    for step in range(3):
        sent = [parts[0] if len(parts) == 1 else jnp.concatenate(parts) for parts in held]
        if extra:
            sent[SIDE] = jnp.concatenate(held[SIDE] + [extra_sum]) if step else thirds[SIDE]
        if hook is not None:
            hook(step, sent)
        got = [move(value, **order[step][0]) for value, order in zip(sent, links)]
        held = [parts + [value] for parts, value in zip(held, got)]
        if extra:
            held[SIDE][-1] = got[SIDE][:-extra]
            extra_sum = add_all(extra_sum, got[SIDE][-extra:])
    return [array for pair in zip(sent, got) for array in pair]


def add_all(*terms):
    total = terms[0].astype(F32)
    for term in terms[1:]:
        total = total + term.astype(F32)
    return total.astype(BF16)


def collect(parts, links, extra=0):
    held = [[part] for part in parts[0::2]]
    sent = list(parts[1::2])
    extra_sum = sent[SIDE][-extra:]
    for step in range(3):
        got = [move(value, **order[2 - step][0]) for value, order in zip(sent, links)]
        added = list(got)
        if extra:
            extra_sum = add_all(extra_sum, got[SIDE][-extra:])
            added[SIDE] = got[SIDE][:-extra]
        held = [terms + [value] for terms, value in zip(held, added)]
        if step < 2:
            half = [terms[0].shape[0] // 2 for terms in held]
            sent = [add_all(*[t[h:] for t in terms]) for terms, h in zip(held, half)]
            held = [[t[:h] for t in terms] for terms, h in zip(held, half)]
            if extra:
                sent[SIDE] = jnp.concatenate([sent[SIDE], extra_sum])
    total = jnp.concatenate([add_all(*terms) for terms in held])
    return (total, extra_sum) if extra else total


def vmem_spec():
    return pl.BlockSpec(memory_space=pltpu.VMEM)


def smem_spec():
    return pl.BlockSpec(memory_space=pltpu.SMEM)


def any_spec():
    return pl.BlockSpec(memory_space=pl.ANY)


def hbm_spec():
    return pl.BlockSpec(memory_space=pltpu.HBM)


def cost(flops, moved):
    return pl.CostEstimate(flops=flops, bytes_accessed=moved, transcendentals=0)


def third_shapes(pieces=1, extra=0):
    counts = [pieces * (hi - lo) for lo, hi in CUTS]
    counts[SIDE] += extra
    return [jax.ShapeDtypeStruct((count, TILE, TILE), BF16) for count in counts]


def third_of(tile):
    return next((at, tile - lo) for at, (lo, hi) in enumerate(CUTS) if lo <= tile < hi)


def turn_kernel(core_ref, own_ref, sib_ref, *out_refs):
    lanes = pl.ds(pl.multiple_of(core_ref[0] * TILE, TILE), TILE)
    for half, ref in enumerate((own_ref, sib_ref)):
        for tile in range(8):
            third, at = third_of(half * 8 + tile)
            out_refs[third][at] = ref[tile * TILE : (tile + 1) * TILE, lanes].T


def turn_in(core, own, sib):
    return pl.pallas_call(
        turn_kernel,
        out_shape=third_shapes(),
        in_specs=[smem_spec(), vmem_spec(), vmem_spec()],
        out_specs=[vmem_spec()] * 3,
        compiler_params=pltpu.CompilerParams(vmem_limit_bytes=8 << 20),
        cost_estimate=cost(0, 2 << 20),
        name="turn_in",
    )(core, own, sib)


def array_place(ids):
    mark, tile = ids // 16, ids % 16
    turn, other = mark // 2, mark % 2
    near = ((turn == 1) | (turn == 2)).astype(jnp.int32)
    far = (turn >= 2).astype(jnp.int32)
    bits = ((near, far, other), (far, other, near), (other, near, far))
    array, row = jnp.zeros_like(ids), jnp.zeros_like(ids)
    for third, ((lo, hi), (a, b, c)) in enumerate(zip(CUTS, bits)):
        here = (tile >= lo) & (tile < hi)
        array = jnp.where(here, 2 * third + c, array)
        row = jnp.where(here, (a + 2 * b) * (hi - lo) + tile - lo, row)
    return array, row


def total_row(ids):
    array, row = array_place(ids)
    first = sum(jnp.where(array // 2 == third, 4 * lo, 0) for third, (lo, _) in enumerate(CUTS))
    return first + row + 64 * (1 - array % 2)


def order_slots(source_ids, target_ids, dead):
    array, row = array_place(source_ids)
    target = total_row(target_ids)
    late = jnp.where(target < 64, 3, 6)
    key = jnp.where(dead, 9, array // 2 + jnp.where(array % 2 == 1, late, 0)).reshape(-1)
    at = jnp.arange(key.shape[0], dtype=jnp.int32)
    packed = (row + 32 * target).reshape(-1) + 4096 * at
    ahead = (key[None, :] < key[:, None]) | (
        (key[None, :] == key[:, None]) & (at[None, :] < at[:, None])
    )
    rank = jnp.sum(ahead.astype(jnp.int32), axis=1)
    listed = jnp.sum(jnp.where(rank[None, :] == at[:, None], packed[None, :], 0), axis=1)
    marks = jnp.arange(10, dtype=jnp.int32)[:, None]
    bounds = jnp.sum((key[None, :] < marks).astype(jnp.int32), axis=1)
    return listed, bounds


def add_products(adjoint, first_class, list_ref, bound_ref, sources, tiles, total, base=0):
    dims = (((1,), (0,)), ((), ())) if adjoint else (((1,), (1,)), ((), ()))
    final, unused = tiles.shape[0] - 1, total.shape[0] - 1
    for index, source in enumerate(sources):
        first, last = bound_ref[first_class + index], bound_ref[first_class + index + 1]

        @pl.loop(0, lax.div(last - first + (GROUP - 1), GROUP))
        def _(group, source=source, first=first, last=last):
            products, places_to = [], []
            for step in range(GROUP):
                at = first + group * GROUP + step
                live = at < last
                entry = jnp.where(live, list_ref[jnp.minimum(at, final)], 0)
                places_to.append(jnp.where(live, ((entry >> 5) & 127) - base, unused))
                products.append(
                    lax.dot_general(
                        source[entry & 31],
                        tiles[entry >> 12],
                        dims,
                        preferred_element_type=F32,
                    )
                )
            for to, product in zip(places_to, products):
                total[to] = total[to] + product


def clear(total):
    @pl.loop(0, total.shape[0] // 3)
    def _(at):
        total[pl.ds(at * 3, 3)] = jnp.zeros((3,) + total.shape[1:], F32)


def give(total, result):
    @pl.loop(0, 32)
    def _(at):
        result[pl.ds(at * 4, 4)] = total[pl.ds(at * 4, 4)].astype(BF16)


def load_kernel(live_ref, list_ref, bound_ref, own_tiles, sib_tiles, *rest):
    sources, (result, tiles, total, sems) = rest[:3], rest[3:]
    slots = own_tiles.shape[0]
    lists = (own_tiles, sib_tiles)
    groups = [lax.div(live_ref[side] + (LOAD - 1), LOAD) for side in range(2)]

    def tile_copy(side, group):
        first = pl.multiple_of(group * LOAD, LOAD)
        return pltpu.make_async_copy(
            lists[side].at[pl.ds(first, LOAD)],
            tiles.at[pl.ds(side * slots + first, LOAD)],
            sems.at[side, group],
        )

    for side in range(2):
        pl.loop(0, groups[side])(lambda group, side=side: tile_copy(side, group).start())
    clear(total)
    for side in range(2):
        pl.loop(0, groups[side])(lambda group, side=side: tile_copy(side, group).wait())
    add_products(False, 0, list_ref, bound_ref, sources, tiles, total)
    give(total, result)


def early_kernel(list_ref, bound_ref, tiles, *rest):
    sources, (result, total) = rest[:3], rest[3:]
    clear(total)
    add_products(True, 0, list_ref, bound_ref, sources, tiles, total)
    give(total, result)


def late_kernel(adjoint, kept, list_ref, bound_ref, tiles, before, *rest):
    sources, rest = rest[:3], rest[3:]
    if adjoint and not kept:
        extra_ref, *rest = rest
        rows = extra_ref.shape[0] - EXTRA, extra_ref.shape[0]
        extra = extra_ref[rows[0] : rows[1]].astype(F32) + sources[SIDE][rows[0] : rows[1]].astype(F32)
        rest[SIDE][rows[0] : rows[1]] = extra.astype(BF16)
    *targets, total = rest
    base = 64 if kept else 0

    @pl.loop(0, 16)
    def _(at):
        total[pl.ds(at * 4, 4)] = before[pl.ds(base + at * 4, 4)].astype(F32)

    add_products(
        adjoint, 6 if kept else 3, list_ref, bound_ref, sources, tiles, total, base
    )
    for target, (lo, hi) in zip(targets, CUTS):
        for row in range(4 * (hi - lo)):
            target[row] = total[4 * lo + row].astype(BF16)


TOTAL = jax.ShapeDtypeStruct((128, TILE, TILE), BF16)
SUMS = pltpu.VMEM((129, TILE, TILE), F32)


def pass_params():
    return pltpu.CompilerParams(vmem_limit_bytes=PASS_VMEM << 20)


def early_pass(adjoint, live, listed, bounds, tiles, sources):
    estimate = cost(128 * TILE * TILE * TILE, 16 << 20)
    if adjoint:
        return tiles, pl.pallas_call(
            early_kernel,
            out_shape=TOTAL,
            in_specs=[smem_spec()] * 2 + [vmem_spec()] * 4,
            out_specs=vmem_spec(),
            scratch_shapes=[SUMS],
            compiler_params=pass_params(),
            cost_estimate=estimate,
            name="early_adjoint",
        )(listed, bounds, tiles, *sources)
    slots = tiles[0].shape[0]
    total, tiles = pl.pallas_call(
        load_kernel,
        out_shape=[TOTAL, jax.ShapeDtypeStruct((2 * slots, TILE, TILE), BF16)],
        in_specs=[smem_spec()] * 3 + [any_spec()] * 2 + [vmem_spec()] * 3,
        out_specs=[vmem_spec()] * 2,
        scratch_shapes=[SUMS, pltpu.SemaphoreType.DMA((2, slots // LOAD))],
        compiler_params=pass_params(),
        cost_estimate=estimate,
        name="early_pass",
    )(live, listed, bounds, *tiles, *sources)
    return tiles, total


def late_pass(adjoint, kept, listed, bounds, tiles, total, sources, extra=()):
    return pl.pallas_call(
        functools.partial(late_kernel, adjoint, kept),
        out_shape=third_shapes(4, EXTRA if extra else 0),
        in_specs=[smem_spec()] * 2 + [vmem_spec()] * (5 + len(extra)),
        out_specs=[vmem_spec()] * 3,
        scratch_shapes=[pltpu.VMEM((65, TILE, TILE), F32)],
        compiler_params=pass_params(),
        cost_estimate=cost(64 * TILE * TILE * TILE, 8 << 20),
        name=("kept" if kept else "sent") + ("_adjoint" if adjoint else "_pass"),
    )(listed, bounds, tiles, total, *sources, *extra)


def block_pass(adjoint, live, order, tiles, sources):
    extra = sources[2 * SIDE : 2 * SIDE + 1] if adjoint else ()
    tiles, total = early_pass(adjoint, live, *order, tiles, sources[0::2])
    sent = late_pass(adjoint, False, *order, tiles, total, sources[1::2], extra)
    held = late_pass(adjoint, True, *order, tiles, total, sources[1::2])
    return [array for pair in zip(held, sent) for array in pair], tiles


def dense_pair(weights, half, tile, cot_ref, own_sums, sib_sums):
    own = [own_sums[half * 8 + tile + step] for step in range(2)]
    sib = [sib_sums[(1 - half) * 8 + tile + step] for step in range(2)]
    nodes = [jnp.concatenate([a.T, b.T], axis=1) for a, b in zip(own, sib)]
    pre = jnp.dot(jnp.concatenate(nodes), weights, preferred_element_type=F32)
    sigmoid = 0.5 * jnp.tanh(0.5 * pre) + 0.5
    slope = sigmoid * (1.0 + pre * (1.0 - sigmoid))
    cot = cot_ref[tile * TILE : (tile + 2) * TILE, :]
    grad = (cot.astype(F32) * slope).astype(BF16)
    wgrad = jnp.dot(jnp.concatenate(own, axis=1), grad, preferred_element_type=F32)
    mixed = lax.dot_general(
        weights[:TILE], grad, (((1,), (1,)), ((), ())), preferred_element_type=F32
    ).astype(BF16)
    return (pre * sigmoid).astype(BF16), wgrad, (mixed[:, :TILE], mixed[:, TILE:])


def ordered_weight(core_ref, weight_ref):
    core = core_ref[0]
    halves = [pl.ds(pl.multiple_of(at * TILE, TILE), TILE) for at in (core, 1 - core)]
    return jnp.concatenate([weight_ref[half, :] for half in halves])


def dense_kernel(core_ref, weight_ref, own_cot, sib_cot, own_sums, sib_sums, act_ref, *mixed_refs):
    weights = ordered_weight(core_ref, weight_ref)
    total = None
    for at in range(0, 16, 2):
        half, tile = divmod(at, 8)
        cot = sib_cot if half else own_cot
        act, wgrad, mixed = dense_pair(weights, half, tile, cot, own_sums, sib_sums)
        if not half:
            act_ref[tile * TILE : (tile + 2) * TILE, :] = act
        total = wgrad if total is None else total + wgrad
        for step, value in enumerate(mixed):
            third, place = third_of(at + step)
            mixed_refs[third][place] = value
    for part in range(EXTRA):
        extra = total[:, part * TILE : (part + 1) * TILE]
        mixed_refs[SIDE][CUTS[SIDE][1] - CUTS[SIDE][0] + part] = extra.astype(BF16)


def dense(core, weight, own_cot, sib_cot, own_sums, sib_sums):
    act, *mixed = pl.pallas_call(
        dense_kernel,
        out_shape=[jax.ShapeDtypeStruct(own_cot.shape, BF16)] + third_shapes(1, EXTRA),
        in_specs=[smem_spec()] + [vmem_spec()] * 5,
        out_specs=[vmem_spec()] * 4,
        compiler_params=pltpu.CompilerParams(vmem_limit_bytes=24 << 20),
        cost_estimate=cost(2 * 2048 * 256 * 512, 4 << 20),
        name="dense",
    )(core, weight, own_cot, sib_cot, own_sums, sib_sums)
    return act, mixed


def back_kernel(core_ref, own_ref, sib_ref, out_ref):
    core = core_ref[0]
    for ref, half in ((own_ref, core), (sib_ref, 1 - core)):
        lanes = pl.ds(pl.multiple_of(half * TILE, TILE), TILE)
        for tile in range(8):
            out_ref[tile * TILE : (tile + 1) * TILE, lanes] = ref[tile].T


def turn_back(core, own_part, sib_part):
    return pl.pallas_call(
        back_kernel,
        out_shape=jax.ShapeDtypeStruct((8 * TILE, 2 * TILE), BF16),
        in_specs=[smem_spec()] + [vmem_spec()] * 2,
        out_specs=vmem_spec(),
        compiler_params=pltpu.CompilerParams(vmem_limit_bytes=8 << 20),
        cost_estimate=cost(0, 1 << 20),
        name="turn_back",
    )(core, own_part, sib_part)


def body(features, weight, cotangent, blocks, block_row, block_col, counts):
    row_at, col_at = lax.axis_index("gr"), lax.axis_index("gc")
    y, xl, core = row_at // 4, (row_at // 2) % 2, row_at % 2
    xh, z = col_at // 4, col_at % 4
    core_arg = core.reshape(1).astype(jnp.int32)

    sib_feats = move(features, core=1)
    slices = turn_in(core_arg, features, sib_feats)

    own_tiles = blocks[0, 0]
    slots = own_tiles.shape[0]
    fetched = []

    def fetch(step, sent):
        if step == 2:
            event = sent[2]
            live = jnp.broadcast_to(after(counts[0, 0], event), (slots,))
            rows, cols = after(block_row[0, 0], event), after(block_col[0, 0], event)
            lists = jnp.stack([rows, cols, live])
            fetched.extend([lists, move(lists, core=1), move(after(cotangent, event), core=1)])

    gathered = spread(slices, GR_LINKS, fetch)
    own_lists, sib_lists, sib_cot = fetched
    sib_tiles = move(after(own_tiles, slices[0]), core=1)
    lists = jnp.stack([own_lists, sib_lists], axis=1)
    rows, cols, live = lists[0], lists[1], lists[2, :, 0]
    side = jnp.arange(2, dtype=jnp.int32)[:, None]
    part = rows // 8
    row_ids = (((part % 4) ^ z) * 2 + ((part // 4) ^ xh)) * 16 + side * 8 + rows % 8
    part = cols // 8
    col_ids = ((part // 4) ^ y) * 32 + (((part // 2) % 2) ^ xl) * 16
    col_ids = col_ids + ((part % 2) ^ core) * 8 + cols % 8
    dead = jnp.arange(slots, dtype=jnp.int32)[None, :] >= live[:, None]
    by_col = order_slots(col_ids, row_ids, dead)
    by_col = (after(by_col[0], sib_cot), by_col[1])
    by_row = order_slots(row_ids, col_ids, dead)

    parts, tiles = block_pass(False, live, by_col, (own_tiles, sib_tiles), gathered)
    own_sums = collect(parts, GC_LINKS)
    sib_sums = move(own_sums, core=1)

    activations, mixed = dense(core_arg, weight, cotangent, sib_cot, own_sums, sib_sums)

    gathered = spread(mixed, GC_LINKS, extra=EXTRA)
    parts, _ = block_pass(True, live, by_row, tiles, gathered)
    grads, wgrad = collect(parts, GR_LINKS, EXTRA)
    last = move(jnp.concatenate([grads[8:], wgrad]), core=1)
    feature_grad = turn_back(core_arg, grads[:8], last)

    node_total = features.shape[0] * lax.axis_size("gr") * lax.axis_size("gc")
    halves = [jnp.concatenate([part[-2], part[-1]], axis=1).astype(F32) for part in (wgrad, last)]
    weight_grad = jnp.where(core == 0, jnp.concatenate(halves), jnp.concatenate(halves[::-1]))
    weight_grad = weight_grad * (1.0 / math.sqrt(node_total))
    return (activations, weight_grad, feature_grad)


def solution(mesh):
    return jax.shard_map(
        body,
        mesh=mesh,
        in_specs=(
            P(("gr", "gc"), None),
            P(),
            P(("gr", "gc"), None),
            P("gr", "gc", None, None, None),
            P("gr", "gc", None),
            P("gr", "gc", None),
            P("gr", "gc"),
        ),
        out_specs=(P(("gr", "gc"), None), P(), P(("gr", "gc"), None)),
        check_vma=False,
    )
```

```python
import functools
import math

import jax
import jax.numpy as jnp
from jax import lax
from jax.experimental import pallas as pl
from jax.experimental.pallas import tpu as pltpu
from jax.sharding import PartitionSpec as P

AXES = ("gr", "gc")
TILE = 128
CUTS = ((0, 6), (6, 11), (11, 16))
SIDE = 1
EXTRA = 2
NODES = 131072
GROUP = 8
LOAD = 8
PASS_VMEM = 26
F32 = jnp.float32
BF16 = jnp.bfloat16


def split_place(index):
    row, col = divmod(index, 8)
    y, rest = divmod(row, 4)
    xl, core = divmod(rest, 2)
    xh, z = divmod(col, 4)
    return y, xl, core, xh, z


def join_place(y, xl, core, xh, z):
    return ((y % 4) * 4 + (xl % 2) * 2 + core % 2) * 8 + (xh % 2) * 4 + z % 4


def move(value, y=0, xl=0, core=0, xh=0, z=0):
    masks = (y, xl, core, xh, z)
    pairs = []
    for index in range(128):
        at = split_place(index)
        pairs.append((index, join_place(*(a ^ b for a, b in zip(at, masks)))))
    return lax.ppermute(value, AXES, pairs)


def link_orders(ring, pair):
    near, far, other = (1, 0), (3, 0), (0, 1)
    orders = ((near, far, other), (far, other, near), (other, near, far))
    return [[({ring: r, pair: p}, r * 2 + p) for r, p in order] for order in orders]


def places(order):
    marks = [mark for _, mark in order]
    return [
        (marks[0] if p & 1 else 0) ^ (marks[1] if p & 2 else 0) ^ (marks[2] if p & 4 else 0)
        for p in range(8)
    ]


GR_LINKS = link_orders("y", "xl")
GC_LINKS = link_orders("z", "xh")


def after(value, *earlier):
    return lax.optimization_barrier((value,) + earlier)[0]


def spread(thirds, links, hook=None, extra=0):
    held = [[third] for third in thirds]
    if extra:
        held[SIDE], extra_sum = [thirds[SIDE][:-extra]], thirds[SIDE][-extra:]
    for step in range(3):
        sent = [parts[0] if len(parts) == 1 else jnp.concatenate(parts) for parts in held]
        if extra:
            sent[SIDE] = jnp.concatenate(held[SIDE] + [extra_sum]) if step else thirds[SIDE]
        if hook is not None:
            hook(step, sent)
        got = [move(value, **order[step][0]) for value, order in zip(sent, links)]
        held = [parts + [value] for parts, value in zip(held, got)]
        if extra:
            held[SIDE][-1] = got[SIDE][:-extra]
            extra_sum = add_all(extra_sum, got[SIDE][-extra:])
    return [array for pair in zip(sent, got) for array in pair]


def add_all(*terms):
    total = terms[0].astype(F32)
    for term in terms[1:]:
        total = total + term.astype(F32)
    return total.astype(BF16)


def collect(parts, links, extra=0):
    held = [[part] for part in parts[0::2]]
    sent = list(parts[1::2])
    extra_sum = sent[SIDE][-extra:]
    for step in range(3):
        got = [move(value, **order[2 - step][0]) for value, order in zip(sent, links)]
        added = list(got)
        if extra:
            extra_sum = add_all(extra_sum, got[SIDE][-extra:])
            added[SIDE] = got[SIDE][:-extra]
        held = [terms + [value] for terms, value in zip(held, added)]
        if step < 2:
            half = [terms[0].shape[0] // 2 for terms in held]
            sent = [add_all(*[t[h:] for t in terms]) for terms, h in zip(held, half)]
            held = [[t[:h] for t in terms] for terms, h in zip(held, half)]
            if extra:
                sent[SIDE] = jnp.concatenate([sent[SIDE], extra_sum])
    total = jnp.concatenate([add_all(*terms) for terms in held])
    return (total, extra_sum) if extra else total


def vmem_spec():
    return pl.BlockSpec(memory_space=pltpu.VMEM)


def smem_spec():
    return pl.BlockSpec(memory_space=pltpu.SMEM)


def any_spec():
    return pl.BlockSpec(memory_space=pl.ANY)


def hbm_spec():
    return pl.BlockSpec(memory_space=pltpu.HBM)


def cost(flops, moved):
    return pl.CostEstimate(flops=flops, bytes_accessed=moved, transcendentals=0)


def third_shapes(pieces=1, extra=0):
    counts = [pieces * (hi - lo) for lo, hi in CUTS]
    counts[SIDE] += extra
    return [jax.ShapeDtypeStruct((count, TILE, TILE), BF16) for count in counts]


def third_of(tile):
    return next((at, tile - lo) for at, (lo, hi) in enumerate(CUTS) if lo <= tile < hi)


def turn_kernel(core_ref, own_ref, sib_ref, *out_refs):
    lanes = pl.ds(pl.multiple_of(core_ref[0] * TILE, TILE), TILE)
    for half, ref in enumerate((own_ref, sib_ref)):
        for tile in range(8):
            third, at = third_of(half * 8 + tile)
            out_refs[third][at] = ref[tile * TILE : (tile + 1) * TILE, lanes].T


def turn_in(core, own, sib):
    return pl.pallas_call(
        turn_kernel,
        out_shape=third_shapes(),
        in_specs=[smem_spec(), vmem_spec(), vmem_spec()],
        out_specs=[vmem_spec()] * 3,
        compiler_params=pltpu.CompilerParams(vmem_limit_bytes=8 << 20),
        cost_estimate=cost(0, 2 << 20),
        name="turn_in",
    )(core, own, sib)


def array_place(ids):
    mark, tile = ids // 16, ids % 16
    turn, other = mark // 2, mark % 2
    near = ((turn == 1) | (turn == 2)).astype(jnp.int32)
    far = (turn >= 2).astype(jnp.int32)
    bits = ((near, far, other), (far, other, near), (other, near, far))
    array, row = jnp.zeros_like(ids), jnp.zeros_like(ids)
    for third, ((lo, hi), (a, b, c)) in enumerate(zip(CUTS, bits)):
        here = (tile >= lo) & (tile < hi)
        array = jnp.where(here, 2 * third + c, array)
        row = jnp.where(here, (a + 2 * b) * (hi - lo) + tile - lo, row)
    return array, row


def total_row(ids):
    array, row = array_place(ids)
    first = sum(jnp.where(array // 2 == third, 4 * lo, 0) for third, (lo, _) in enumerate(CUTS))
    return first + row + 64 * (1 - array % 2)


def order_slots(source_ids, target_ids, dead):
    array, row = array_place(source_ids)
    target = total_row(target_ids)
    late = jnp.where(target < 64, 3, 6)
    key = jnp.where(dead, 9, array // 2 + jnp.where(array % 2 == 1, late, 0)).reshape(-1)
    at = jnp.arange(key.shape[0], dtype=jnp.int32)
    packed = (row + 32 * target).reshape(-1) + 4096 * at
    ahead = (key[None, :] < key[:, None]) | (
        (key[None, :] == key[:, None]) & (at[None, :] < at[:, None])
    )
    rank = jnp.sum(ahead.astype(jnp.int32), axis=1)
    listed = jnp.sum(jnp.where(rank[None, :] == at[:, None], packed[None, :], 0), axis=1)
    marks = jnp.arange(10, dtype=jnp.int32)[:, None]
    bounds = jnp.sum((key[None, :] < marks).astype(jnp.int32), axis=1)
    return listed, bounds


def add_products(adjoint, first_class, list_ref, bound_ref, sources, tiles, total, base=0):
    dims = (((1,), (0,)), ((), ())) if adjoint else (((1,), (1,)), ((), ()))
    final, unused = tiles.shape[0] - 1, total.shape[0] - 1
    for index, source in enumerate(sources):
        first, last = bound_ref[first_class + index], bound_ref[first_class + index + 1]

        @pl.loop(0, lax.div(last - first + (GROUP - 1), GROUP))
        def _(group, source=source, first=first, last=last):
            products, places_to = [], []
            for step in range(GROUP):
                at = first + group * GROUP + step
                live = at < last
                entry = jnp.where(live, list_ref[jnp.minimum(at, final)], 0)
                places_to.append(jnp.where(live, ((entry >> 5) & 127) - base, unused))
                products.append(
                    lax.dot_general(
                        source[entry & 31],
                        tiles[entry >> 12],
                        dims,
                        preferred_element_type=F32,
                    )
                )
            for to, product in zip(places_to, products):
                total[to] = total[to] + product


def clear(total):
    @pl.loop(0, total.shape[0] // 3)
    def _(at):
        total[pl.ds(at * 3, 3)] = jnp.zeros((3,) + total.shape[1:], F32)


def give(total, result):
    @pl.loop(0, 32)
    def _(at):
        result[pl.ds(at * 4, 4)] = total[pl.ds(at * 4, 4)].astype(BF16)


def load_kernel(live_ref, list_ref, bound_ref, own_tiles, sib_tiles, *rest):
    sources, (result, tiles, total, sems) = rest[:3], rest[3:]
    slots = own_tiles.shape[0]
    lists = (own_tiles, sib_tiles)
    groups = [lax.div(live_ref[side] + (LOAD - 1), LOAD) for side in range(2)]

    def tile_copy(side, group):
        first = pl.multiple_of(group * LOAD, LOAD)
        return pltpu.make_async_copy(
            lists[side].at[pl.ds(first, LOAD)],
            tiles.at[pl.ds(side * slots + first, LOAD)],
            sems.at[side, group],
        )

    for side in range(2):
        pl.loop(0, groups[side])(lambda group, side=side: tile_copy(side, group).start())
    clear(total)
    for side in range(2):
        pl.loop(0, groups[side])(lambda group, side=side: tile_copy(side, group).wait())
    add_products(False, 0, list_ref, bound_ref, sources, tiles, total)
    give(total, result)


def early_kernel(list_ref, bound_ref, tiles, *rest):
    sources, (result, total) = rest[:3], rest[3:]
    clear(total)
    add_products(True, 0, list_ref, bound_ref, sources, tiles, total)
    give(total, result)


def late_kernel(adjoint, kept, list_ref, bound_ref, tiles, before, *rest):
    sources, rest = rest[:3], rest[3:]
    if adjoint and not kept:
        extra_ref, *rest = rest
        rows = extra_ref.shape[0] - EXTRA, extra_ref.shape[0]
        extra = extra_ref[rows[0] : rows[1]].astype(F32) + sources[SIDE][rows[0] : rows[1]].astype(F32)
        rest[SIDE][rows[0] : rows[1]] = extra.astype(BF16)
    *targets, total = rest
    base = 64 if kept else 0

    @pl.loop(0, 16)
    def _(at):
        total[pl.ds(at * 4, 4)] = before[pl.ds(base + at * 4, 4)].astype(F32)

    add_products(
        adjoint, 6 if kept else 3, list_ref, bound_ref, sources, tiles, total, base
    )
    for target, (lo, hi) in zip(targets, CUTS):
        for row in range(4 * (hi - lo)):
            target[row] = total[4 * lo + row].astype(BF16)


TOTAL = jax.ShapeDtypeStruct((128, TILE, TILE), BF16)
SUMS = pltpu.VMEM((129, TILE, TILE), F32)


def pass_params():
    return pltpu.CompilerParams(vmem_limit_bytes=PASS_VMEM << 20)


def early_pass(adjoint, live, listed, bounds, tiles, sources):
    estimate = cost(128 * TILE * TILE * TILE, 16 << 20)
    if adjoint:
        return tiles, pl.pallas_call(
            early_kernel,
            out_shape=TOTAL,
            in_specs=[smem_spec()] * 2 + [vmem_spec()] * 4,
            out_specs=vmem_spec(),
            scratch_shapes=[SUMS],
            compiler_params=pass_params(),
            cost_estimate=estimate,
            name="early_adjoint",
        )(listed, bounds, tiles, *sources)
    slots = tiles[0].shape[0]
    total, tiles = pl.pallas_call(
        load_kernel,
        out_shape=[TOTAL, jax.ShapeDtypeStruct((2 * slots, TILE, TILE), BF16)],
        in_specs=[smem_spec()] * 3 + [any_spec()] * 2 + [vmem_spec()] * 3,
        out_specs=[vmem_spec()] * 2,
        scratch_shapes=[SUMS, pltpu.SemaphoreType.DMA((2, slots // LOAD))],
        compiler_params=pass_params(),
        cost_estimate=estimate,
        name="early_pass",
    )(live, listed, bounds, *tiles, *sources)
    return tiles, total


def late_pass(adjoint, kept, listed, bounds, tiles, total, sources, extra=()):
    return pl.pallas_call(
        functools.partial(late_kernel, adjoint, kept),
        out_shape=third_shapes(4, EXTRA if extra else 0),
        in_specs=[smem_spec()] * 2 + [vmem_spec()] * (5 + len(extra)),
        out_specs=[vmem_spec()] * 3,
        scratch_shapes=[pltpu.VMEM((65, TILE, TILE), F32)],
        compiler_params=pass_params(),
        cost_estimate=cost(64 * TILE * TILE * TILE, 8 << 20),
        name=("kept" if kept else "sent") + ("_adjoint" if adjoint else "_pass"),
    )(listed, bounds, tiles, total, *sources, *extra)


def block_pass(adjoint, live, order, tiles, sources):
    extra = sources[2 * SIDE : 2 * SIDE + 1] if adjoint else ()
    tiles, total = early_pass(adjoint, live, *order, tiles, sources[0::2])
    sent = late_pass(adjoint, False, *order, tiles, total, sources[1::2], extra)
    held = late_pass(adjoint, True, *order, tiles, total, sources[1::2])
    return [array for pair in zip(held, sent) for array in pair], tiles


def dense_pair(weights, half, tile, cot_ref, own_sums, sib_sums):
    own = [own_sums[half * 8 + tile + step] for step in range(2)]
    sib = [sib_sums[(1 - half) * 8 + tile + step] for step in range(2)]
    nodes = [jnp.concatenate([a.T, b.T], axis=1) for a, b in zip(own, sib)]
    pre = jnp.dot(jnp.concatenate(nodes), weights, preferred_element_type=F32)
    sigmoid = 0.5 * jnp.tanh(0.5 * pre) + 0.5
    slope = sigmoid * (1.0 + pre * (1.0 - sigmoid))
    cot = cot_ref[tile * TILE : (tile + 2) * TILE, :]
    grad = (cot.astype(F32) * slope).astype(BF16)
    wgrad = jnp.dot(jnp.concatenate(own, axis=1), grad, preferred_element_type=F32)
    mixed = lax.dot_general(
        weights[:TILE], grad, (((1,), (1,)), ((), ())), preferred_element_type=F32
    ).astype(BF16)
    return (pre * sigmoid).astype(BF16), wgrad, (mixed[:, :TILE], mixed[:, TILE:])


def ordered_weight(core_ref, weight_ref):
    core = core_ref[0]
    halves = [pl.ds(pl.multiple_of(at * TILE, TILE), TILE) for at in (core, 1 - core)]
    return jnp.concatenate([weight_ref[half, :] for half in halves])


def dense_kernel(core_ref, weight_ref, own_cot, sib_cot, own_sums, sib_sums, act_ref, *mixed_refs):
    weights = ordered_weight(core_ref, weight_ref)
    total = None
    for at in range(0, 16, 2):
        half, tile = divmod(at, 8)
        cot = sib_cot if half else own_cot
        act, wgrad, mixed = dense_pair(weights, half, tile, cot, own_sums, sib_sums)
        if not half:
            act_ref[tile * TILE : (tile + 2) * TILE, :] = act
        total = wgrad if total is None else total + wgrad
        for step, value in enumerate(mixed):
            third, place = third_of(at + step)
            mixed_refs[third][place] = value
    for part in range(EXTRA):
        extra = total[:, part * TILE : (part + 1) * TILE]
        mixed_refs[SIDE][CUTS[SIDE][1] - CUTS[SIDE][0] + part] = extra.astype(BF16)


def dense(core, weight, own_cot, sib_cot, own_sums, sib_sums):
    act, *mixed = pl.pallas_call(
        dense_kernel,
        out_shape=[jax.ShapeDtypeStruct(own_cot.shape, BF16)] + third_shapes(1, EXTRA),
        in_specs=[smem_spec()] + [vmem_spec()] * 5,
        out_specs=[vmem_spec()] * 4,
        compiler_params=pltpu.CompilerParams(vmem_limit_bytes=24 << 20),
        cost_estimate=cost(2 * 2048 * 256 * 512, 4 << 20),
        name="dense",
    )(core, weight, own_cot, sib_cot, own_sums, sib_sums)
    return act, mixed


def back_kernel(core_ref, own_ref, sib_ref, wgrad_ref, out_ref, weight_ref):
    core = core_ref[0]
    scale = 1.0 / math.sqrt(NODES)
    extra = sib_ref.shape[0] - EXTRA
    for ref, half in ((own_ref, core), (sib_ref, 1 - core)):
        lanes = pl.ds(pl.multiple_of(half * TILE, TILE), TILE)
        for tile in range(8):
            out_ref[tile * TILE : (tile + 1) * TILE, lanes] = ref[tile].T
    for ref, first, half in ((wgrad_ref, 0, core), (sib_ref, extra, 1 - core)):
        rows = pl.ds(pl.multiple_of(half * TILE, TILE), TILE)
        for part in range(EXTRA):
            lanes = slice(part * TILE, (part + 1) * TILE)
            weight_ref[rows, lanes] = ref[first + part].astype(F32) * scale


def turn_back(core, own_part, sib_part, wgrad):
    return pl.pallas_call(
        back_kernel,
        out_shape=[
            jax.ShapeDtypeStruct((8 * TILE, 2 * TILE), BF16),
            jax.ShapeDtypeStruct((2 * TILE, 2 * TILE), F32),
        ],
        in_specs=[smem_spec()] + [vmem_spec()] * 3,
        out_specs=[vmem_spec()] * 2,
        compiler_params=pltpu.CompilerParams(vmem_limit_bytes=8 << 20),
        cost_estimate=cost(0, 1 << 20),
        name="turn_back",
    )(core, own_part, sib_part, wgrad)


def body(features, weight, cotangent, blocks, block_row, block_col, counts):
    row_at, col_at = lax.axis_index("gr"), lax.axis_index("gc")
    y, xl, core = row_at // 4, (row_at // 2) % 2, row_at % 2
    xh, z = col_at // 4, col_at % 4
    core_arg = core.reshape(1).astype(jnp.int32)

    sib_feats = move(features, core=1)
    slices = turn_in(core_arg, features, sib_feats)

    own_tiles = blocks[0, 0]
    slots = own_tiles.shape[0]
    fetched = []

    def fetch(step, sent):
        if step == 2:
            event = sent[2]
            live = jnp.broadcast_to(after(counts[0, 0], event), (slots,))
            rows, cols = after(block_row[0, 0], event), after(block_col[0, 0], event)
            lists = jnp.stack([rows, cols, live])
            fetched.extend([lists, move(lists, core=1), move(after(cotangent, event), core=1)])

    gathered = spread(slices, GR_LINKS, fetch)
    own_lists, sib_lists, sib_cot = fetched
    sib_tiles = move(after(own_tiles, slices[0]), core=1)
    lists = jnp.stack([own_lists, sib_lists], axis=1)
    rows, cols, live = lists[0], lists[1], lists[2, :, 0]
    side = jnp.arange(2, dtype=jnp.int32)[:, None]
    part = rows // 8
    row_ids = (((part % 4) ^ z) * 2 + ((part // 4) ^ xh)) * 16 + side * 8 + rows % 8
    part = cols // 8
    col_ids = ((part // 4) ^ y) * 32 + (((part // 2) % 2) ^ xl) * 16
    col_ids = col_ids + ((part % 2) ^ core) * 8 + cols % 8
    dead = jnp.arange(slots, dtype=jnp.int32)[None, :] >= live[:, None]
    by_col = order_slots(col_ids, row_ids, dead)
    by_col = (after(by_col[0], sib_cot), by_col[1])
    by_row = order_slots(row_ids, col_ids, dead)

    parts, tiles = block_pass(False, live, by_col, (own_tiles, sib_tiles), gathered)
    own_sums = collect(parts, GC_LINKS)
    sib_sums = move(own_sums, core=1)

    activations, mixed = dense(core_arg, weight, cotangent, sib_cot, own_sums, sib_sums)

    gathered = spread(mixed, GC_LINKS, extra=EXTRA)
    parts, _ = block_pass(True, live, by_row, tiles, gathered)
    grads, wgrad = collect(parts, GR_LINKS, EXTRA)
    last = move(jnp.concatenate([grads[8:], wgrad]), core=1)
    feature_grad, weight_grad = turn_back(core_arg, grads[:8], last, wgrad)
    return (activations, weight_grad, feature_grad)


def solution(mesh):
    return jax.shard_map(
        body,
        mesh=mesh,
        in_specs=(
            P(("gr", "gc"), None),
            P(),
            P(("gr", "gc"), None),
            P("gr", "gc", None, None, None),
            P("gr", "gc", None),
            P("gr", "gc", None),
            P("gr", "gc"),
        ),
        out_specs=(P(("gr", "gc"), None), P(), P(("gr", "gc"), None)),
        check_vma=False,
    )
```

```python
import functools
import math

import jax
import jax.numpy as jnp
from jax import lax
from jax.experimental import pallas as pl
from jax.experimental.pallas import tpu as pltpu
from jax.sharding import PartitionSpec as P

AXES = ("gr", "gc")
TILE = 128
CUTS = ((0, 6), (6, 11), (11, 16))
SIDE = 1
EXTRA = 2
NODES = 131072
GROUP = 8
LOAD = 8
PASS_VMEM = 26
F32 = jnp.float32
BF16 = jnp.bfloat16


def split_place(index):
    row, col = divmod(index, 8)
    y, rest = divmod(row, 4)
    xl, core = divmod(rest, 2)
    xh, z = divmod(col, 4)
    return y, xl, core, xh, z


def join_place(y, xl, core, xh, z):
    return ((y % 4) * 4 + (xl % 2) * 2 + core % 2) * 8 + (xh % 2) * 4 + z % 4


def move(value, y=0, xl=0, core=0, xh=0, z=0):
    masks = (y, xl, core, xh, z)
    pairs = []
    for index in range(128):
        at = split_place(index)
        pairs.append((index, join_place(*(a ^ b for a, b in zip(at, masks)))))
    return lax.ppermute(value, AXES, pairs)


def link_orders(ring, pair):
    near, far, other = (1, 0), (3, 0), (0, 1)
    orders = ((near, far, other), (far, other, near), (other, near, far))
    return [[({ring: r, pair: p}, r * 2 + p) for r, p in order] for order in orders]


def places(order):
    marks = [mark for _, mark in order]
    return [
        (marks[0] if p & 1 else 0) ^ (marks[1] if p & 2 else 0) ^ (marks[2] if p & 4 else 0)
        for p in range(8)
    ]


GR_LINKS = link_orders("y", "xl")
GC_LINKS = link_orders("z", "xh")


def after(value, *earlier):
    return lax.optimization_barrier((value,) + earlier)[0]


def spread(thirds, links, hook=None, extra=0):
    held = [[third] for third in thirds]
    if extra:
        held[SIDE], extra_sum = [thirds[SIDE][:-extra]], thirds[SIDE][-extra:]
    for step in range(3):
        sent = [parts[0] if len(parts) == 1 else jnp.concatenate(parts) for parts in held]
        if extra:
            sent[SIDE] = jnp.concatenate(held[SIDE] + [extra_sum]) if step else thirds[SIDE]
        if hook is not None:
            hook(step, sent)
        got = [move(value, **order[step][0]) for value, order in zip(sent, links)]
        held = [parts + [value] for parts, value in zip(held, got)]
        if extra:
            held[SIDE][-1] = got[SIDE][:-extra]
            extra_sum = add_all(extra_sum, got[SIDE][-extra:])
    return [array for pair in zip(sent, got) for array in pair]


def add_all(*terms):
    total = terms[0].astype(F32)
    for term in terms[1:]:
        total = total + term.astype(F32)
    return total.astype(BF16)


def collect(parts, links, extra=0):
    held = [[part] for part in parts[0::2]]
    sent = list(parts[1::2])
    extra_sum = sent[SIDE][-extra:]
    for step in range(3):
        got = [move(value, **order[2 - step][0]) for value, order in zip(sent, links)]
        added = list(got)
        if extra:
            extra_sum = add_all(extra_sum, got[SIDE][-extra:])
            added[SIDE] = got[SIDE][:-extra]
        held = [terms + [value] for terms, value in zip(held, added)]
        if step < 2:
            half = [terms[0].shape[0] // 2 for terms in held]
            sent = [add_all(*[t[h:] for t in terms]) for terms, h in zip(held, half)]
            held = [[t[:h] for t in terms] for terms, h in zip(held, half)]
            if extra:
                sent[SIDE] = jnp.concatenate([sent[SIDE], extra_sum])
    total = jnp.concatenate([add_all(*terms) for terms in held])
    return (total, extra_sum) if extra else total


def vmem_spec():
    return pl.BlockSpec(memory_space=pltpu.VMEM)


def smem_spec():
    return pl.BlockSpec(memory_space=pltpu.SMEM)


def any_spec():
    return pl.BlockSpec(memory_space=pl.ANY)


def hbm_spec():
    return pl.BlockSpec(memory_space=pltpu.HBM)


def cost(flops, moved):
    return pl.CostEstimate(flops=flops, bytes_accessed=moved, transcendentals=0)


def third_shapes(pieces=1, extra=0):
    counts = [pieces * (hi - lo) for lo, hi in CUTS]
    counts[SIDE] += extra
    return [jax.ShapeDtypeStruct((count, TILE, TILE), BF16) for count in counts]


def third_of(tile):
    return next((at, tile - lo) for at, (lo, hi) in enumerate(CUTS) if lo <= tile < hi)


def turn_kernel(core_ref, own_any, sib_ref, *rest):
    out_refs, (own_ref, sem) = rest[:3], rest[3:]
    load = pltpu.make_async_copy(own_any, own_ref, sem)
    load.start()
    load.wait()
    lanes = pl.ds(pl.multiple_of(core_ref[0] * TILE, TILE), TILE)
    for half, ref in enumerate((own_ref, sib_ref)):
        for tile in range(8):
            third, at = third_of(half * 8 + tile)
            out_refs[third][at] = ref[tile * TILE : (tile + 1) * TILE, lanes].T


def turn_in(core, own, sib):
    return pl.pallas_call(
        turn_kernel,
        out_shape=third_shapes(),
        in_specs=[smem_spec(), any_spec(), vmem_spec()],
        out_specs=[vmem_spec()] * 3,
        scratch_shapes=[pltpu.VMEM(own.shape, BF16), pltpu.SemaphoreType.DMA],
        compiler_params=pltpu.CompilerParams(vmem_limit_bytes=8 << 20),
        cost_estimate=cost(0, 2 << 20),
        name="turn_in",
    )(core, own, sib)


def array_place(ids):
    mark, tile = ids // 16, ids % 16
    turn, other = mark // 2, mark % 2
    near = ((turn == 1) | (turn == 2)).astype(jnp.int32)
    far = (turn >= 2).astype(jnp.int32)
    bits = ((near, far, other), (far, other, near), (other, near, far))
    array, row = jnp.zeros_like(ids), jnp.zeros_like(ids)
    for third, ((lo, hi), (a, b, c)) in enumerate(zip(CUTS, bits)):
        here = (tile >= lo) & (tile < hi)
        array = jnp.where(here, 2 * third + c, array)
        row = jnp.where(here, (a + 2 * b) * (hi - lo) + tile - lo, row)
    return array, row


def total_row(ids):
    array, row = array_place(ids)
    first = sum(jnp.where(array // 2 == third, 4 * lo, 0) for third, (lo, _) in enumerate(CUTS))
    return first + row + 64 * (1 - array % 2)


def order_slots(source_ids, target_ids, dead):
    array, row = array_place(source_ids)
    target = total_row(target_ids)
    late = jnp.where(target < 64, 3, 6)
    key = jnp.where(dead, 9, array // 2 + jnp.where(array % 2 == 1, late, 0)).reshape(-1)
    at = jnp.arange(key.shape[0], dtype=jnp.int32)
    packed = (row + 32 * target).reshape(-1) + 4096 * at
    ahead = (key[None, :] < key[:, None]) | (
        (key[None, :] == key[:, None]) & (at[None, :] < at[:, None])
    )
    rank = jnp.sum(ahead.astype(jnp.int32), axis=1)
    listed = jnp.sum(jnp.where(rank[None, :] == at[:, None], packed[None, :], 0), axis=1)
    marks = jnp.arange(10, dtype=jnp.int32)[:, None]
    bounds = jnp.sum((key[None, :] < marks).astype(jnp.int32), axis=1)
    return listed, bounds


def add_products(adjoint, first_class, list_ref, bound_ref, sources, tiles, total, base=0):
    dims = (((1,), (0,)), ((), ())) if adjoint else (((1,), (1,)), ((), ()))
    final, unused = tiles.shape[0] - 1, total.shape[0] - 1
    for index, source in enumerate(sources):
        first, last = bound_ref[first_class + index], bound_ref[first_class + index + 1]

        @pl.loop(0, lax.div(last - first + (GROUP - 1), GROUP))
        def _(group, source=source, first=first, last=last):
            products, places_to = [], []
            for step in range(GROUP):
                at = first + group * GROUP + step
                live = at < last
                entry = jnp.where(live, list_ref[jnp.minimum(at, final)], 0)
                places_to.append(jnp.where(live, ((entry >> 5) & 127) - base, unused))
                products.append(
                    lax.dot_general(
                        source[entry & 31],
                        tiles[entry >> 12],
                        dims,
                        preferred_element_type=F32,
                    )
                )
            for to, product in zip(places_to, products):
                total[to] = total[to] + product


def clear(total):
    @pl.loop(0, total.shape[0] // 3)
    def _(at):
        total[pl.ds(at * 3, 3)] = jnp.zeros((3,) + total.shape[1:], F32)


def give(total, result):
    @pl.loop(0, 32)
    def _(at):
        result[pl.ds(at * 4, 4)] = total[pl.ds(at * 4, 4)].astype(BF16)


def load_kernel(live_ref, list_ref, bound_ref, own_tiles, sib_tiles, *rest):
    sources, (result, tiles, total, sems) = rest[:3], rest[3:]
    slots = own_tiles.shape[0]
    lists = (own_tiles, sib_tiles)
    groups = [lax.div(live_ref[side] + (LOAD - 1), LOAD) for side in range(2)]

    def tile_copy(side, group):
        first = pl.multiple_of(group * LOAD, LOAD)
        return pltpu.make_async_copy(
            lists[side].at[pl.ds(first, LOAD)],
            tiles.at[pl.ds(side * slots + first, LOAD)],
            sems.at[side, group],
        )

    for side in range(2):
        pl.loop(0, groups[side])(lambda group, side=side: tile_copy(side, group).start())
    clear(total)
    for side in range(2):
        pl.loop(0, groups[side])(lambda group, side=side: tile_copy(side, group).wait())
    add_products(False, 0, list_ref, bound_ref, sources, tiles, total)
    give(total, result)


def early_kernel(list_ref, bound_ref, tiles, *rest):
    sources, (result, total) = rest[:3], rest[3:]
    clear(total)
    add_products(True, 0, list_ref, bound_ref, sources, tiles, total)
    give(total, result)


def late_kernel(adjoint, kept, list_ref, bound_ref, tiles, before, *rest):
    sources, rest = rest[:3], rest[3:]
    if adjoint and not kept:
        extra_ref, *rest = rest
        rows = extra_ref.shape[0] - EXTRA, extra_ref.shape[0]
        extra = extra_ref[rows[0] : rows[1]].astype(F32) + sources[SIDE][rows[0] : rows[1]].astype(F32)
        rest[SIDE][rows[0] : rows[1]] = extra.astype(BF16)
    *targets, total = rest
    base = 64 if kept else 0

    @pl.loop(0, 16)
    def _(at):
        total[pl.ds(at * 4, 4)] = before[pl.ds(base + at * 4, 4)].astype(F32)

    add_products(
        adjoint, 6 if kept else 3, list_ref, bound_ref, sources, tiles, total, base
    )
    for target, (lo, hi) in zip(targets, CUTS):
        for row in range(4 * (hi - lo)):
            target[row] = total[4 * lo + row].astype(BF16)


TOTAL = jax.ShapeDtypeStruct((128, TILE, TILE), BF16)
SUMS = pltpu.VMEM((129, TILE, TILE), F32)


def pass_params():
    return pltpu.CompilerParams(vmem_limit_bytes=PASS_VMEM << 20)


def early_pass(adjoint, live, listed, bounds, tiles, sources):
    estimate = cost(128 * TILE * TILE * TILE, 16 << 20)
    if adjoint:
        return tiles, pl.pallas_call(
            early_kernel,
            out_shape=TOTAL,
            in_specs=[smem_spec()] * 2 + [vmem_spec()] * 4,
            out_specs=vmem_spec(),
            scratch_shapes=[SUMS],
            compiler_params=pass_params(),
            cost_estimate=estimate,
            name="early_adjoint",
        )(listed, bounds, tiles, *sources)
    slots = tiles[0].shape[0]
    total, tiles = pl.pallas_call(
        load_kernel,
        out_shape=[TOTAL, jax.ShapeDtypeStruct((2 * slots, TILE, TILE), BF16)],
        in_specs=[smem_spec()] * 3 + [any_spec()] * 2 + [vmem_spec()] * 3,
        out_specs=[vmem_spec()] * 2,
        scratch_shapes=[SUMS, pltpu.SemaphoreType.DMA((2, slots // LOAD))],
        compiler_params=pass_params(),
        cost_estimate=estimate,
        name="early_pass",
    )(live, listed, bounds, *tiles, *sources)
    return tiles, total


def late_pass(adjoint, kept, listed, bounds, tiles, total, sources, extra=()):
    return pl.pallas_call(
        functools.partial(late_kernel, adjoint, kept),
        out_shape=third_shapes(4, EXTRA if extra else 0),
        in_specs=[smem_spec()] * 2 + [vmem_spec()] * (5 + len(extra)),
        out_specs=[vmem_spec()] * 3,
        scratch_shapes=[pltpu.VMEM((65, TILE, TILE), F32)],
        compiler_params=pass_params(),
        cost_estimate=cost(64 * TILE * TILE * TILE, 8 << 20),
        name=("kept" if kept else "sent") + ("_adjoint" if adjoint else "_pass"),
    )(listed, bounds, tiles, total, *sources, *extra)


def block_pass(adjoint, live, order, tiles, sources):
    extra = sources[2 * SIDE : 2 * SIDE + 1] if adjoint else ()
    tiles, total = early_pass(adjoint, live, *order, tiles, sources[0::2])
    sent = late_pass(adjoint, False, *order, tiles, total, sources[1::2], extra)
    held = late_pass(adjoint, True, *order, tiles, total, sources[1::2])
    return [array for pair in zip(held, sent) for array in pair], tiles


def dense_pair(weights, half, tile, cot_ref, own_sums, sib_sums):
    own = [own_sums[half * 8 + tile + step] for step in range(2)]
    sib = [sib_sums[(1 - half) * 8 + tile + step] for step in range(2)]
    nodes = [jnp.concatenate([a.T, b.T], axis=1) for a, b in zip(own, sib)]
    pre = jnp.dot(jnp.concatenate(nodes), weights, preferred_element_type=F32)
    sigmoid = 0.5 * jnp.tanh(0.5 * pre) + 0.5
    slope = sigmoid * (1.0 + pre * (1.0 - sigmoid))
    cot = cot_ref[tile * TILE : (tile + 2) * TILE, :]
    grad = (cot.astype(F32) * slope).astype(BF16)
    wgrad = jnp.dot(jnp.concatenate(own, axis=1), grad, preferred_element_type=F32)
    mixed = lax.dot_general(
        weights[:TILE], grad, (((1,), (1,)), ((), ())), preferred_element_type=F32
    ).astype(BF16)
    return (pre * sigmoid).astype(BF16), wgrad, (mixed[:, :TILE], mixed[:, TILE:])


def ordered_weight(core_ref, weight_ref):
    core = core_ref[0]
    halves = [pl.ds(pl.multiple_of(at * TILE, TILE), TILE) for at in (core, 1 - core)]
    return jnp.concatenate([weight_ref[half, :] for half in halves])


def dense_kernel(core_ref, weight_ref, own_cot, sib_cot, own_sums, sib_sums, act_ref, *mixed_refs):
    weights = ordered_weight(core_ref, weight_ref)
    total = None
    for at in range(0, 16, 2):
        half, tile = divmod(at, 8)
        cot = sib_cot if half else own_cot
        act, wgrad, mixed = dense_pair(weights, half, tile, cot, own_sums, sib_sums)
        if not half:
            act_ref[tile * TILE : (tile + 2) * TILE, :] = act
        total = wgrad if total is None else total + wgrad
        for step, value in enumerate(mixed):
            third, place = third_of(at + step)
            mixed_refs[third][place] = value
    for part in range(EXTRA):
        extra = total[:, part * TILE : (part + 1) * TILE]
        mixed_refs[SIDE][CUTS[SIDE][1] - CUTS[SIDE][0] + part] = extra.astype(BF16)


def dense(core, weight, own_cot, sib_cot, own_sums, sib_sums):
    act, *mixed = pl.pallas_call(
        dense_kernel,
        out_shape=[jax.ShapeDtypeStruct(own_cot.shape, BF16)] + third_shapes(1, EXTRA),
        in_specs=[smem_spec()] + [vmem_spec()] * 5,
        out_specs=[vmem_spec()] * 4,
        compiler_params=pltpu.CompilerParams(vmem_limit_bytes=24 << 20),
        cost_estimate=cost(2 * 2048 * 256 * 512, 4 << 20),
        name="dense",
    )(core, weight, own_cot, sib_cot, own_sums, sib_sums)
    return act, mixed


def back_kernel(core_ref, own_ref, sib_ref, wgrad_ref, out_ref, weight_ref):
    core = core_ref[0]
    scale = 1.0 / math.sqrt(NODES)
    extra = sib_ref.shape[0] - EXTRA
    for ref, half in ((own_ref, core), (sib_ref, 1 - core)):
        lanes = pl.ds(pl.multiple_of(half * TILE, TILE), TILE)
        for tile in range(8):
            out_ref[tile * TILE : (tile + 1) * TILE, lanes] = ref[tile].T
    for ref, first, half in ((wgrad_ref, 0, core), (sib_ref, extra, 1 - core)):
        rows = pl.ds(pl.multiple_of(half * TILE, TILE), TILE)
        for part in range(EXTRA):
            lanes = slice(part * TILE, (part + 1) * TILE)
            weight_ref[rows, lanes] = ref[first + part].astype(F32) * scale


def turn_back(core, own_part, sib_part, wgrad):
    return pl.pallas_call(
        back_kernel,
        out_shape=[
            jax.ShapeDtypeStruct((8 * TILE, 2 * TILE), BF16),
            jax.ShapeDtypeStruct((2 * TILE, 2 * TILE), F32),
        ],
        in_specs=[smem_spec()] + [vmem_spec()] * 3,
        out_specs=[vmem_spec()] * 2,
        compiler_params=pltpu.CompilerParams(vmem_limit_bytes=8 << 20),
        cost_estimate=cost(0, 1 << 20),
        name="turn_back",
    )(core, own_part, sib_part, wgrad)


def body(features, weight, cotangent, blocks, block_row, block_col, counts):
    row_at, col_at = lax.axis_index("gr"), lax.axis_index("gc")
    y, xl, core = row_at // 4, (row_at // 2) % 2, row_at % 2
    xh, z = col_at // 4, col_at % 4
    core_arg = core.reshape(1).astype(jnp.int32)

    sib_feats = move(features, core=1)
    slices = turn_in(core_arg, features, sib_feats)

    own_tiles = blocks[0, 0]
    slots = own_tiles.shape[0]
    fetched = []

    def fetch(step, sent):
        if step == 2:
            event = sent[2]
            live = jnp.broadcast_to(after(counts[0, 0], event), (slots,))
            rows, cols = after(block_row[0, 0], event), after(block_col[0, 0], event)
            lists = jnp.stack([rows, cols, live])
            fetched.extend([lists, move(lists, core=1), move(after(cotangent, event), core=1)])

    gathered = spread(slices, GR_LINKS, fetch)
    own_lists, sib_lists, sib_cot = fetched
    sib_tiles = move(after(own_tiles, slices[0]), core=1)
    lists = jnp.stack([own_lists, sib_lists], axis=1)
    rows, cols, live = lists[0], lists[1], lists[2, :, 0]
    side = jnp.arange(2, dtype=jnp.int32)[:, None]
    part = rows // 8
    row_ids = (((part % 4) ^ z) * 2 + ((part // 4) ^ xh)) * 16 + side * 8 + rows % 8
    part = cols // 8
    col_ids = ((part // 4) ^ y) * 32 + (((part // 2) % 2) ^ xl) * 16
    col_ids = col_ids + ((part % 2) ^ core) * 8 + cols % 8
    dead = jnp.arange(slots, dtype=jnp.int32)[None, :] >= live[:, None]
    by_col = order_slots(col_ids, row_ids, dead)
    by_col = (after(by_col[0], sib_cot), by_col[1])
    by_row = order_slots(row_ids, col_ids, dead)

    parts, tiles = block_pass(False, live, by_col, (own_tiles, sib_tiles), gathered)
    own_sums = collect(parts, GC_LINKS)
    sib_sums = move(own_sums, core=1)

    activations, mixed = dense(core_arg, weight, cotangent, sib_cot, own_sums, sib_sums)

    gathered = spread(mixed, GC_LINKS, extra=EXTRA)
    parts, _ = block_pass(True, live, by_row, tiles, gathered)
    grads, wgrad = collect(parts, GR_LINKS, EXTRA)
    last = move(jnp.concatenate([grads[8:], wgrad]), core=1)
    feature_grad, weight_grad = turn_back(core_arg, grads[:8], last, wgrad)
    return (activations, weight_grad, feature_grad)


def solution(mesh):
    return jax.shard_map(
        body,
        mesh=mesh,
        in_specs=(
            P(("gr", "gc"), None),
            P(),
            P(("gr", "gc"), None),
            P("gr", "gc", None, None, None),
            P("gr", "gc", None),
            P("gr", "gc", None),
            P("gr", "gc"),
        ),
        out_specs=(P(("gr", "gc"), None), P(), P(("gr", "gc"), None)),
        check_vma=False,
    )
```

```python
import functools
import math

import jax
import jax.numpy as jnp
from jax import lax
from jax.experimental import pallas as pl
from jax.experimental.pallas import tpu as pltpu
from jax.sharding import PartitionSpec as P

AXES = ("gr", "gc")
TILE = 128
CUTS = ((0, 6), (6, 11), (11, 16))
SIDE = 1
EXTRA = 2
NODES = 131072
GROUP = 8
LOAD = 8
PASS_VMEM = 26
F32 = jnp.float32
BF16 = jnp.bfloat16


def split_place(index):
    row, col = divmod(index, 8)
    y, rest = divmod(row, 4)
    xl, core = divmod(rest, 2)
    xh, z = divmod(col, 4)
    return y, xl, core, xh, z


def join_place(y, xl, core, xh, z):
    return ((y % 4) * 4 + (xl % 2) * 2 + core % 2) * 8 + (xh % 2) * 4 + z % 4


def move(value, y=0, xl=0, core=0, xh=0, z=0):
    masks = (y, xl, core, xh, z)
    pairs = []
    for index in range(128):
        at = split_place(index)
        pairs.append((index, join_place(*(a ^ b for a, b in zip(at, masks)))))
    return lax.ppermute(value, AXES, pairs)


def link_orders(ring, pair):
    near, far, other = (1, 0), (3, 0), (0, 1)
    orders = ((far, other, near), (other, near, far), (near, far, other))
    return [[({ring: r, pair: p}, r * 2 + p) for r, p in order] for order in orders]


def places(order):
    marks = [mark for _, mark in order]
    return [
        (marks[0] if p & 1 else 0) ^ (marks[1] if p & 2 else 0) ^ (marks[2] if p & 4 else 0)
        for p in range(8)
    ]


GR_LINKS = link_orders("y", "xl")
GC_LINKS = link_orders("z", "xh")


def after(value, *earlier):
    return lax.optimization_barrier((value,) + earlier)[0]


def spread(thirds, links, hook=None, extra=0):
    held = [[third] for third in thirds]
    if extra:
        held[SIDE], extra_sum = [thirds[SIDE][:-extra]], thirds[SIDE][-extra:]
    for step in range(3):
        sent = [parts[0] if len(parts) == 1 else jnp.concatenate(parts) for parts in held]
        if extra:
            sent[SIDE] = jnp.concatenate(held[SIDE] + [extra_sum]) if step else thirds[SIDE]
        if hook is not None:
            hook(step, sent)
        got = [move(value, **order[step][0]) for value, order in zip(sent, links)]
        held = [parts + [value] for parts, value in zip(held, got)]
        if extra:
            held[SIDE][-1] = got[SIDE][:-extra]
            extra_sum = add_all(extra_sum, got[SIDE][-extra:])
    return [array for pair in zip(sent, got) for array in pair]


def add_all(*terms):
    total = terms[0].astype(F32)
    for term in terms[1:]:
        total = total + term.astype(F32)
    return total.astype(BF16)


def collect(parts, links, extra=0):
    held = [[part] for part in parts[0::2]]
    sent = list(parts[1::2])
    extra_sum = sent[SIDE][-extra:]
    for step in range(3):
        got = [move(value, **order[2 - step][0]) for value, order in zip(sent, links)]
        added = list(got)
        if extra:
            extra_sum = add_all(extra_sum, got[SIDE][-extra:])
            added[SIDE] = got[SIDE][:-extra]
        held = [terms + [value] for terms, value in zip(held, added)]
        if step < 2:
            half = [terms[0].shape[0] // 2 for terms in held]
            sent = [add_all(*[t[h:] for t in terms]) for terms, h in zip(held, half)]
            held = [[t[:h] for t in terms] for terms, h in zip(held, half)]
            if extra:
                sent[SIDE] = jnp.concatenate([sent[SIDE], extra_sum])
    total = jnp.concatenate([add_all(*terms) for terms in held])
    return (total, extra_sum) if extra else total


def vmem_spec():
    return pl.BlockSpec(memory_space=pltpu.VMEM)


def smem_spec():
    return pl.BlockSpec(memory_space=pltpu.SMEM)


def any_spec():
    return pl.BlockSpec(memory_space=pl.ANY)


def hbm_spec():
    return pl.BlockSpec(memory_space=pltpu.HBM)


def cost(flops, moved):
    return pl.CostEstimate(flops=flops, bytes_accessed=moved, transcendentals=0)


def third_shapes(pieces=1, extra=0):
    counts = [pieces * (hi - lo) for lo, hi in CUTS]
    counts[SIDE] += extra
    return [jax.ShapeDtypeStruct((count, TILE, TILE), BF16) for count in counts]


def third_of(tile):
    return next((at, tile - lo) for at, (lo, hi) in enumerate(CUTS) if lo <= tile < hi)


def turn_kernel(core_ref, own_ref, sib_ref, *out_refs):
    lanes = pl.ds(pl.multiple_of(core_ref[0] * TILE, TILE), TILE)
    for half, ref in enumerate((own_ref, sib_ref)):
        for tile in range(8):
            third, at = third_of(half * 8 + tile)
            out_refs[third][at] = ref[tile * TILE : (tile + 1) * TILE, lanes].T


def turn_in(core, own, sib):
    return pl.pallas_call(
        turn_kernel,
        out_shape=third_shapes(),
        in_specs=[smem_spec(), vmem_spec(), vmem_spec()],
        out_specs=[vmem_spec()] * 3,
        compiler_params=pltpu.CompilerParams(vmem_limit_bytes=8 << 20),
        cost_estimate=cost(0, 2 << 20),
        name="turn_in",
    )(core, own, sib)


def array_place(ids):
    mark, tile = ids // 16, ids % 16
    turn, other = mark // 2, mark % 2
    near = ((turn == 1) | (turn == 2)).astype(jnp.int32)
    far = (turn >= 2).astype(jnp.int32)
    bits = ((far, other, near), (other, near, far), (near, far, other))
    array, row = jnp.zeros_like(ids), jnp.zeros_like(ids)
    for third, ((lo, hi), (a, b, c)) in enumerate(zip(CUTS, bits)):
        here = (tile >= lo) & (tile < hi)
        array = jnp.where(here, 2 * third + c, array)
        row = jnp.where(here, (a + 2 * b) * (hi - lo) + tile - lo, row)
    return array, row


def total_row(ids):
    array, row = array_place(ids)
    first = sum(jnp.where(array // 2 == third, 4 * lo, 0) for third, (lo, _) in enumerate(CUTS))
    return first + row + 64 * (1 - array % 2)


def order_slots(source_ids, target_ids, dead):
    array, row = array_place(source_ids)
    target = total_row(target_ids)
    late = jnp.where(target < 64, 3, 6)
    key = jnp.where(dead, 9, array // 2 + jnp.where(array % 2 == 1, late, 0)).reshape(-1)
    at = jnp.arange(key.shape[0], dtype=jnp.int32)
    packed = (row + 32 * target).reshape(-1) + 4096 * at
    ahead = (key[None, :] < key[:, None]) | (
        (key[None, :] == key[:, None]) & (at[None, :] < at[:, None])
    )
    rank = jnp.sum(ahead.astype(jnp.int32), axis=1)
    listed = jnp.sum(jnp.where(rank[None, :] == at[:, None], packed[None, :], 0), axis=1)
    marks = jnp.arange(10, dtype=jnp.int32)[:, None]
    bounds = jnp.sum((key[None, :] < marks).astype(jnp.int32), axis=1)
    return listed, bounds


def add_products(adjoint, first_class, list_ref, bound_ref, sources, tiles, total, base=0):
    dims = (((1,), (0,)), ((), ())) if adjoint else (((1,), (1,)), ((), ()))
    final, unused = tiles.shape[0] - 1, total.shape[0] - 1
    for index, source in enumerate(sources):
        first, last = bound_ref[first_class + index], bound_ref[first_class + index + 1]

        @pl.loop(0, lax.div(last - first + (GROUP - 1), GROUP))
        def _(group, source=source, first=first, last=last):
            products, places_to = [], []
            for step in range(GROUP):
                at = first + group * GROUP + step
                live = at < last
                entry = jnp.where(live, list_ref[jnp.minimum(at, final)], 0)
                places_to.append(jnp.where(live, ((entry >> 5) & 127) - base, unused))
                products.append(
                    lax.dot_general(
                        source[entry & 31],
                        tiles[entry >> 12],
                        dims,
                        preferred_element_type=F32,
                    )
                )
            for to, product in zip(places_to, products):
                total[to] = total[to] + product


def clear(total):
    @pl.loop(0, total.shape[0] // 3)
    def _(at):
        total[pl.ds(at * 3, 3)] = jnp.zeros((3,) + total.shape[1:], F32)


def give(total, result):
    @pl.loop(0, 32)
    def _(at):
        result[pl.ds(at * 4, 4)] = total[pl.ds(at * 4, 4)].astype(BF16)


def load_kernel(live_ref, list_ref, bound_ref, own_tiles, sib_tiles, *rest):
    sources, (result, tiles, total, sems) = rest[:3], rest[3:]
    slots = own_tiles.shape[0]
    lists = (own_tiles, sib_tiles)
    groups = [lax.div(live_ref[side] + (LOAD - 1), LOAD) for side in range(2)]

    def tile_copy(side, group):
        first = pl.multiple_of(group * LOAD, LOAD)
        return pltpu.make_async_copy(
            lists[side].at[pl.ds(first, LOAD)],
            tiles.at[pl.ds(side * slots + first, LOAD)],
            sems.at[side, group],
        )

    for side in range(2):
        pl.loop(0, groups[side])(lambda group, side=side: tile_copy(side, group).start())
    clear(total)
    for side in range(2):
        pl.loop(0, groups[side])(lambda group, side=side: tile_copy(side, group).wait())
    add_products(False, 0, list_ref, bound_ref, sources, tiles, total)
    give(total, result)


def early_kernel(list_ref, bound_ref, tiles, *rest):
    sources, (result, total) = rest[:3], rest[3:]
    clear(total)
    add_products(True, 0, list_ref, bound_ref, sources, tiles, total)
    give(total, result)


def late_kernel(adjoint, kept, list_ref, bound_ref, tiles, before, *rest):
    sources, rest = rest[:3], rest[3:]
    if adjoint and not kept:
        extra_ref, *rest = rest
        rows = extra_ref.shape[0] - EXTRA, extra_ref.shape[0]
        extra = extra_ref[rows[0] : rows[1]].astype(F32) + sources[SIDE][rows[0] : rows[1]].astype(F32)
        rest[SIDE][rows[0] : rows[1]] = extra.astype(BF16)
    *targets, total = rest
    base = 64 if kept else 0

    @pl.loop(0, 16)
    def _(at):
        total[pl.ds(at * 4, 4)] = before[pl.ds(base + at * 4, 4)].astype(F32)

    add_products(
        adjoint, 6 if kept else 3, list_ref, bound_ref, sources, tiles, total, base
    )
    for target, (lo, hi) in zip(targets, CUTS):
        for row in range(4 * (hi - lo)):
            target[row] = total[4 * lo + row].astype(BF16)


TOTAL = jax.ShapeDtypeStruct((128, TILE, TILE), BF16)
SUMS = pltpu.VMEM((129, TILE, TILE), F32)


def pass_params():
    return pltpu.CompilerParams(vmem_limit_bytes=PASS_VMEM << 20)


def early_pass(adjoint, live, listed, bounds, tiles, sources):
    estimate = cost(128 * TILE * TILE * TILE, 16 << 20)
    if adjoint:
        return tiles, pl.pallas_call(
            early_kernel,
            out_shape=TOTAL,
            in_specs=[smem_spec()] * 2 + [vmem_spec()] * 4,
            out_specs=vmem_spec(),
            scratch_shapes=[SUMS],
            compiler_params=pass_params(),
            cost_estimate=estimate,
            name="early_adjoint",
        )(listed, bounds, tiles, *sources)
    slots = tiles[0].shape[0]
    total, tiles = pl.pallas_call(
        load_kernel,
        out_shape=[TOTAL, jax.ShapeDtypeStruct((2 * slots, TILE, TILE), BF16)],
        in_specs=[smem_spec()] * 3 + [any_spec()] * 2 + [vmem_spec()] * 3,
        out_specs=[vmem_spec()] * 2,
        scratch_shapes=[SUMS, pltpu.SemaphoreType.DMA((2, slots // LOAD))],
        compiler_params=pass_params(),
        cost_estimate=estimate,
        name="early_pass",
    )(live, listed, bounds, *tiles, *sources)
    return tiles, total


def late_pass(adjoint, kept, listed, bounds, tiles, total, sources, extra=()):
    return pl.pallas_call(
        functools.partial(late_kernel, adjoint, kept),
        out_shape=third_shapes(4, EXTRA if extra else 0),
        in_specs=[smem_spec()] * 2 + [vmem_spec()] * (5 + len(extra)),
        out_specs=[vmem_spec()] * 3,
        scratch_shapes=[pltpu.VMEM((65, TILE, TILE), F32)],
        compiler_params=pass_params(),
        cost_estimate=cost(64 * TILE * TILE * TILE, 8 << 20),
        name=("kept" if kept else "sent") + ("_adjoint" if adjoint else "_pass"),
    )(listed, bounds, tiles, total, *sources, *extra)


def block_pass(adjoint, live, order, tiles, sources):
    extra = sources[2 * SIDE : 2 * SIDE + 1] if adjoint else ()
    tiles, total = early_pass(adjoint, live, *order, tiles, sources[0::2])
    sent = late_pass(adjoint, False, *order, tiles, total, sources[1::2], extra)
    held = late_pass(adjoint, True, *order, tiles, total, sources[1::2])
    return [array for pair in zip(held, sent) for array in pair], tiles


def dense_pair(weights, half, tile, cot_ref, own_sums, sib_sums):
    own = [own_sums[half * 8 + tile + step] for step in range(2)]
    sib = [sib_sums[(1 - half) * 8 + tile + step] for step in range(2)]
    nodes = [jnp.concatenate([a.T, b.T], axis=1) for a, b in zip(own, sib)]
    pre = jnp.dot(jnp.concatenate(nodes), weights, preferred_element_type=F32)
    sigmoid = 0.5 * jnp.tanh(0.5 * pre) + 0.5
    slope = sigmoid * (1.0 + pre * (1.0 - sigmoid))
    cot = cot_ref[tile * TILE : (tile + 2) * TILE, :]
    grad = (cot.astype(F32) * slope).astype(BF16)
    wgrad = jnp.dot(jnp.concatenate(own, axis=1), grad, preferred_element_type=F32)
    mixed = lax.dot_general(
        weights[:TILE], grad, (((1,), (1,)), ((), ())), preferred_element_type=F32
    ).astype(BF16)
    return (pre * sigmoid).astype(BF16), wgrad, (mixed[:, :TILE], mixed[:, TILE:])


def ordered_weight(core_ref, weight_ref):
    core = core_ref[0]
    halves = [pl.ds(pl.multiple_of(at * TILE, TILE), TILE) for at in (core, 1 - core)]
    return jnp.concatenate([weight_ref[half, :] for half in halves])


def dense_kernel(core_ref, weight_ref, own_cot, sib_cot, own_sums, sib_sums, act_ref, *mixed_refs):
    weights = ordered_weight(core_ref, weight_ref)
    total = None
    for at in range(0, 16, 2):
        half, tile = divmod(at, 8)
        cot = sib_cot if half else own_cot
        act, wgrad, mixed = dense_pair(weights, half, tile, cot, own_sums, sib_sums)
        if not half:
            act_ref[tile * TILE : (tile + 2) * TILE, :] = act
        total = wgrad if total is None else total + wgrad
        for step, value in enumerate(mixed):
            third, place = third_of(at + step)
            mixed_refs[third][place] = value
    for part in range(EXTRA):
        extra = total[:, part * TILE : (part + 1) * TILE]
        mixed_refs[SIDE][CUTS[SIDE][1] - CUTS[SIDE][0] + part] = extra.astype(BF16)


def dense(core, weight, own_cot, sib_cot, own_sums, sib_sums):
    act, *mixed = pl.pallas_call(
        dense_kernel,
        out_shape=[jax.ShapeDtypeStruct(own_cot.shape, BF16)] + third_shapes(1, EXTRA),
        in_specs=[smem_spec()] + [vmem_spec()] * 5,
        out_specs=[vmem_spec()] * 4,
        compiler_params=pltpu.CompilerParams(vmem_limit_bytes=24 << 20),
        cost_estimate=cost(2 * 2048 * 256 * 512, 4 << 20),
        name="dense",
    )(core, weight, own_cot, sib_cot, own_sums, sib_sums)
    return act, mixed


def back_kernel(core_ref, own_ref, sib_ref, wgrad_ref, out_ref, weight_ref):
    core = core_ref[0]
    scale = 1.0 / math.sqrt(NODES)
    extra = sib_ref.shape[0] - EXTRA
    for ref, half in ((own_ref, core), (sib_ref, 1 - core)):
        lanes = pl.ds(pl.multiple_of(half * TILE, TILE), TILE)
        for tile in range(8):
            out_ref[tile * TILE : (tile + 1) * TILE, lanes] = ref[tile].T
    for ref, first, half in ((wgrad_ref, 0, core), (sib_ref, extra, 1 - core)):
        rows = pl.ds(pl.multiple_of(half * TILE, TILE), TILE)
        for part in range(EXTRA):
            lanes = slice(part * TILE, (part + 1) * TILE)
            weight_ref[rows, lanes] = ref[first + part].astype(F32) * scale


def turn_back(core, own_part, sib_part, wgrad):
    return pl.pallas_call(
        back_kernel,
        out_shape=[
            jax.ShapeDtypeStruct((8 * TILE, 2 * TILE), BF16),
            jax.ShapeDtypeStruct((2 * TILE, 2 * TILE), F32),
        ],
        in_specs=[smem_spec()] + [vmem_spec()] * 3,
        out_specs=[vmem_spec()] * 2,
        compiler_params=pltpu.CompilerParams(vmem_limit_bytes=8 << 20),
        cost_estimate=cost(0, 1 << 20),
        name="turn_back",
    )(core, own_part, sib_part, wgrad)


def body(features, weight, cotangent, blocks, block_row, block_col, counts):
    row_at, col_at = lax.axis_index("gr"), lax.axis_index("gc")
    y, xl, core = row_at // 4, (row_at // 2) % 2, row_at % 2
    xh, z = col_at // 4, col_at % 4
    core_arg = core.reshape(1).astype(jnp.int32)

    sib_feats = move(features, core=1)
    slices = turn_in(core_arg, features, sib_feats)

    own_tiles = blocks[0, 0]
    slots = own_tiles.shape[0]
    fetched = []

    def fetch(step, sent):
        if step == 2:
            event = sent[2]
            live = jnp.broadcast_to(after(counts[0, 0], event), (slots,))
            rows, cols = after(block_row[0, 0], event), after(block_col[0, 0], event)
            lists = jnp.stack([rows, cols, live])
            fetched.extend([lists, move(lists, core=1), move(after(cotangent, event), core=1)])

    gathered = spread(slices, GR_LINKS, fetch)
    own_lists, sib_lists, sib_cot = fetched
    sib_tiles = move(after(own_tiles, slices[0]), core=1)
    lists = jnp.stack([own_lists, sib_lists], axis=1)
    rows, cols, live = lists[0], lists[1], lists[2, :, 0]
    side = jnp.arange(2, dtype=jnp.int32)[:, None]
    part = rows // 8
    row_ids = (((part % 4) ^ z) * 2 + ((part // 4) ^ xh)) * 16 + side * 8 + rows % 8
    part = cols // 8
    col_ids = ((part // 4) ^ y) * 32 + (((part // 2) % 2) ^ xl) * 16
    col_ids = col_ids + ((part % 2) ^ core) * 8 + cols % 8
    dead = jnp.arange(slots, dtype=jnp.int32)[None, :] >= live[:, None]
    by_col = order_slots(col_ids, row_ids, dead)
    by_col = (after(by_col[0], sib_cot), by_col[1])
    by_row = order_slots(row_ids, col_ids, dead)

    parts, tiles = block_pass(False, live, by_col, (own_tiles, sib_tiles), gathered)
    own_sums = collect(parts, GC_LINKS)
    sib_sums = move(own_sums, core=1)

    activations, mixed = dense(core_arg, weight, cotangent, sib_cot, own_sums, sib_sums)

    gathered = spread(mixed, GC_LINKS, extra=EXTRA)
    parts, _ = block_pass(True, live, by_row, tiles, gathered)
    grads, wgrad = collect(parts, GR_LINKS, EXTRA)
    last = move(jnp.concatenate([grads[8:], wgrad]), core=1)
    feature_grad, weight_grad = turn_back(core_arg, grads[:8], last, wgrad)
    return (activations, weight_grad, feature_grad)


def solution(mesh):
    return jax.shard_map(
        body,
        mesh=mesh,
        in_specs=(
            P(("gr", "gc"), None),
            P(),
            P(("gr", "gc"), None),
            P("gr", "gc", None, None, None),
            P("gr", "gc", None),
            P("gr", "gc", None),
            P("gr", "gc"),
        ),
        out_specs=(P(("gr", "gc"), None), P(), P(("gr", "gc"), None)),
        check_vma=False,
    )
```

```python
import functools
import math

import jax
import jax.numpy as jnp
from jax import lax
from jax.experimental import pallas as pl
from jax.experimental.pallas import tpu as pltpu
from jax.sharding import PartitionSpec as P

AXES = ("gr", "gc")
TILE = 128
CUTS = ((0, 5), (5, 11), (11, 16))
SIDE = 0
EXTRA = 2
NODES = 131072
GROUP = 8
LOAD = 8
PASS_VMEM = 26
F32 = jnp.float32
BF16 = jnp.bfloat16


def split_place(index):
    row, col = divmod(index, 8)
    y, rest = divmod(row, 4)
    xl, core = divmod(rest, 2)
    xh, z = divmod(col, 4)
    return y, xl, core, xh, z


def join_place(y, xl, core, xh, z):
    return ((y % 4) * 4 + (xl % 2) * 2 + core % 2) * 8 + (xh % 2) * 4 + z % 4


def move(value, y=0, xl=0, core=0, xh=0, z=0):
    masks = (y, xl, core, xh, z)
    pairs = []
    for index in range(128):
        at = split_place(index)
        pairs.append((index, join_place(*(a ^ b for a, b in zip(at, masks)))))
    return lax.ppermute(value, AXES, pairs)


def link_orders(ring, pair):
    near, far, other = (1, 0), (3, 0), (0, 1)
    orders = ((near, far, other), (far, other, near), (other, near, far))
    return [[({ring: r, pair: p}, r * 2 + p) for r, p in order] for order in orders]


def places(order):
    marks = [mark for _, mark in order]
    return [
        (marks[0] if p & 1 else 0) ^ (marks[1] if p & 2 else 0) ^ (marks[2] if p & 4 else 0)
        for p in range(8)
    ]


GR_LINKS = link_orders("y", "xl")
GC_LINKS = link_orders("z", "xh")


def after(value, *earlier):
    return lax.optimization_barrier((value,) + earlier)[0]


def spread(thirds, links, hook=None, extra=0):
    held = [[third] for third in thirds]
    if extra:
        held[SIDE], extra_sum = [thirds[SIDE][:-extra]], thirds[SIDE][-extra:]
    for step in range(3):
        sent = [parts[0] if len(parts) == 1 else jnp.concatenate(parts) for parts in held]
        if extra:
            sent[SIDE] = jnp.concatenate(held[SIDE] + [extra_sum]) if step else thirds[SIDE]
        if hook is not None:
            hook(step, sent)
        got = [move(value, **order[step][0]) for value, order in zip(sent, links)]
        held = [parts + [value] for parts, value in zip(held, got)]
        if extra:
            held[SIDE][-1] = got[SIDE][:-extra]
            extra_sum = add_all(extra_sum, got[SIDE][-extra:])
    return [array for pair in zip(sent, got) for array in pair]


def add_all(*terms):
    total = terms[0].astype(F32)
    for term in terms[1:]:
        total = total + term.astype(F32)
    return total.astype(BF16)


def collect(parts, links, extra=0):
    held = [[part] for part in parts[0::2]]
    sent = list(parts[1::2])
    extra_sum = sent[SIDE][-extra:]
    for step in range(3):
        got = [move(value, **order[2 - step][0]) for value, order in zip(sent, links)]
        added = list(got)
        if extra:
            extra_sum = add_all(extra_sum, got[SIDE][-extra:])
            added[SIDE] = got[SIDE][:-extra]
        held = [terms + [value] for terms, value in zip(held, added)]
        if step < 2:
            half = [terms[0].shape[0] // 2 for terms in held]
            sent = [add_all(*[t[h:] for t in terms]) for terms, h in zip(held, half)]
            held = [[t[:h] for t in terms] for terms, h in zip(held, half)]
            if extra:
                sent[SIDE] = jnp.concatenate([sent[SIDE], extra_sum])
    total = jnp.concatenate([add_all(*terms) for terms in held])
    return (total, extra_sum) if extra else total


def vmem_spec():
    return pl.BlockSpec(memory_space=pltpu.VMEM)


def smem_spec():
    return pl.BlockSpec(memory_space=pltpu.SMEM)


def any_spec():
    return pl.BlockSpec(memory_space=pl.ANY)


def hbm_spec():
    return pl.BlockSpec(memory_space=pltpu.HBM)


def cost(flops, moved):
    return pl.CostEstimate(flops=flops, bytes_accessed=moved, transcendentals=0)


def third_shapes(pieces=1, extra=0):
    counts = [pieces * (hi - lo) for lo, hi in CUTS]
    counts[SIDE] += extra
    return [jax.ShapeDtypeStruct((count, TILE, TILE), BF16) for count in counts]


def third_of(tile):
    return next((at, tile - lo) for at, (lo, hi) in enumerate(CUTS) if lo <= tile < hi)


def turn_kernel(core_ref, own_ref, sib_ref, *out_refs):
    lanes = pl.ds(pl.multiple_of(core_ref[0] * TILE, TILE), TILE)
    for half, ref in enumerate((own_ref, sib_ref)):
        for tile in range(8):
            third, at = third_of(half * 8 + tile)
            out_refs[third][at] = ref[tile * TILE : (tile + 1) * TILE, lanes].T


def turn_in(core, own, sib):
    return pl.pallas_call(
        turn_kernel,
        out_shape=third_shapes(),
        in_specs=[smem_spec(), vmem_spec(), vmem_spec()],
        out_specs=[vmem_spec()] * 3,
        compiler_params=pltpu.CompilerParams(vmem_limit_bytes=8 << 20),
        cost_estimate=cost(0, 2 << 20),
        name="turn_in",
    )(core, own, sib)


def array_place(ids):
    mark, tile = ids // 16, ids % 16
    turn, other = mark // 2, mark % 2
    near = ((turn == 1) | (turn == 2)).astype(jnp.int32)
    far = (turn >= 2).astype(jnp.int32)
    bits = ((near, far, other), (far, other, near), (other, near, far))
    array, row = jnp.zeros_like(ids), jnp.zeros_like(ids)
    for third, ((lo, hi), (a, b, c)) in enumerate(zip(CUTS, bits)):
        here = (tile >= lo) & (tile < hi)
        array = jnp.where(here, 2 * third + c, array)
        row = jnp.where(here, (a + 2 * b) * (hi - lo) + tile - lo, row)
    return array, row


def total_row(ids):
    array, row = array_place(ids)
    first = sum(jnp.where(array // 2 == third, 4 * lo, 0) for third, (lo, _) in enumerate(CUTS))
    return first + row + 64 * (1 - array % 2)


def order_slots(source_ids, target_ids, dead):
    array, row = array_place(source_ids)
    target = total_row(target_ids)
    late = jnp.where(target < 64, 3, 6)
    key = jnp.where(dead, 9, array // 2 + jnp.where(array % 2 == 1, late, 0)).reshape(-1)
    at = jnp.arange(key.shape[0], dtype=jnp.int32)
    packed = (row + 32 * target).reshape(-1) + 4096 * at
    ahead = (key[None, :] < key[:, None]) | (
        (key[None, :] == key[:, None]) & (at[None, :] < at[:, None])
    )
    rank = jnp.sum(ahead.astype(jnp.int32), axis=1)
    listed = jnp.sum(jnp.where(rank[None, :] == at[:, None], packed[None, :], 0), axis=1)
    marks = jnp.arange(10, dtype=jnp.int32)[:, None]
    bounds = jnp.sum((key[None, :] < marks).astype(jnp.int32), axis=1)
    return listed, bounds


def add_products(adjoint, first_class, list_ref, bound_ref, sources, tiles, total, base=0):
    dims = (((1,), (0,)), ((), ())) if adjoint else (((1,), (1,)), ((), ()))
    final, unused = tiles.shape[0] - 1, total.shape[0] - 1
    for index, source in enumerate(sources):
        first, last = bound_ref[first_class + index], bound_ref[first_class + index + 1]

        @pl.loop(0, lax.div(last - first + (GROUP - 1), GROUP))
        def _(group, source=source, first=first, last=last):
            products, places_to = [], []
            for step in range(GROUP):
                at = first + group * GROUP + step
                live = at < last
                entry = jnp.where(live, list_ref[jnp.minimum(at, final)], 0)
                places_to.append(jnp.where(live, ((entry >> 5) & 127) - base, unused))
                products.append(
                    lax.dot_general(
                        source[entry & 31],
                        tiles[entry >> 12],
                        dims,
                        preferred_element_type=F32,
                    )
                )
            for to, product in zip(places_to, products):
                total[to] = total[to] + product


def clear(total):
    @pl.loop(0, total.shape[0] // 3)
    def _(at):
        total[pl.ds(at * 3, 3)] = jnp.zeros((3,) + total.shape[1:], F32)


def give(total, result):
    @pl.loop(0, 32)
    def _(at):
        result[pl.ds(at * 4, 4)] = total[pl.ds(at * 4, 4)].astype(BF16)


def load_kernel(live_ref, list_ref, bound_ref, own_tiles, sib_tiles, *rest):
    sources, (result, tiles, total, sems) = rest[:3], rest[3:]
    slots = own_tiles.shape[0]
    lists = (own_tiles, sib_tiles)
    groups = [lax.div(live_ref[side] + (LOAD - 1), LOAD) for side in range(2)]

    def tile_copy(side, group):
        first = pl.multiple_of(group * LOAD, LOAD)
        return pltpu.make_async_copy(
            lists[side].at[pl.ds(first, LOAD)],
            tiles.at[pl.ds(side * slots + first, LOAD)],
            sems.at[side, group],
        )

    for side in range(2):
        pl.loop(0, groups[side])(lambda group, side=side: tile_copy(side, group).start())
    clear(total)
    for side in range(2):
        pl.loop(0, groups[side])(lambda group, side=side: tile_copy(side, group).wait())
    add_products(False, 0, list_ref, bound_ref, sources, tiles, total)
    give(total, result)


def early_kernel(list_ref, bound_ref, tiles, *rest):
    sources, (result, total) = rest[:3], rest[3:]
    clear(total)
    add_products(True, 0, list_ref, bound_ref, sources, tiles, total)
    give(total, result)


def late_kernel(adjoint, kept, list_ref, bound_ref, tiles, before, *rest):
    sources, rest = rest[:3], rest[3:]
    if adjoint and not kept:
        extra_ref, *rest = rest
        rows = extra_ref.shape[0] - EXTRA, extra_ref.shape[0]
        extra = extra_ref[rows[0] : rows[1]].astype(F32) + sources[SIDE][rows[0] : rows[1]].astype(F32)
        rest[SIDE][rows[0] : rows[1]] = extra.astype(BF16)
    *targets, total = rest
    base = 64 if kept else 0

    @pl.loop(0, 16)
    def _(at):
        total[pl.ds(at * 4, 4)] = before[pl.ds(base + at * 4, 4)].astype(F32)

    add_products(
        adjoint, 6 if kept else 3, list_ref, bound_ref, sources, tiles, total, base
    )
    for target, (lo, hi) in zip(targets, CUTS):
        for row in range(4 * (hi - lo)):
            target[row] = total[4 * lo + row].astype(BF16)


TOTAL = jax.ShapeDtypeStruct((128, TILE, TILE), BF16)
SUMS = pltpu.VMEM((129, TILE, TILE), F32)


def pass_params():
    return pltpu.CompilerParams(vmem_limit_bytes=PASS_VMEM << 20)


def early_pass(adjoint, live, listed, bounds, tiles, sources):
    estimate = cost(128 * TILE * TILE * TILE, 16 << 20)
    if adjoint:
        return tiles, pl.pallas_call(
            early_kernel,
            out_shape=TOTAL,
            in_specs=[smem_spec()] * 2 + [vmem_spec()] * 4,
            out_specs=vmem_spec(),
            scratch_shapes=[SUMS],
            compiler_params=pass_params(),
            cost_estimate=estimate,
            name="early_adjoint",
        )(listed, bounds, tiles, *sources)
    slots = tiles[0].shape[0]
    total, tiles = pl.pallas_call(
        load_kernel,
        out_shape=[TOTAL, jax.ShapeDtypeStruct((2 * slots, TILE, TILE), BF16)],
        in_specs=[smem_spec()] * 3 + [any_spec()] * 2 + [vmem_spec()] * 3,
        out_specs=[vmem_spec()] * 2,
        scratch_shapes=[SUMS, pltpu.SemaphoreType.DMA((2, slots // LOAD))],
        compiler_params=pass_params(),
        cost_estimate=estimate,
        name="early_pass",
    )(live, listed, bounds, *tiles, *sources)
    return tiles, total


def late_pass(adjoint, kept, listed, bounds, tiles, total, sources, extra=()):
    return pl.pallas_call(
        functools.partial(late_kernel, adjoint, kept),
        out_shape=third_shapes(4, EXTRA if extra else 0),
        in_specs=[smem_spec()] * 2 + [vmem_spec()] * (5 + len(extra)),
        out_specs=[vmem_spec()] * 3,
        scratch_shapes=[pltpu.VMEM((65, TILE, TILE), F32)],
        compiler_params=pass_params(),
        cost_estimate=cost(64 * TILE * TILE * TILE, 8 << 20),
        name=("kept" if kept else "sent") + ("_adjoint" if adjoint else "_pass"),
    )(listed, bounds, tiles, total, *sources, *extra)


def block_pass(adjoint, live, order, tiles, sources):
    extra = sources[2 * SIDE : 2 * SIDE + 1] if adjoint else ()
    tiles, total = early_pass(adjoint, live, *order, tiles, sources[0::2])
    sent = late_pass(adjoint, False, *order, tiles, total, sources[1::2], extra)
    held = late_pass(adjoint, True, *order, tiles, total, sources[1::2])
    return [array for pair in zip(held, sent) for array in pair], tiles


def dense_pair(weights, half, tile, cot_ref, own_sums, sib_sums):
    own = [own_sums[half * 8 + tile + step] for step in range(2)]
    sib = [sib_sums[(1 - half) * 8 + tile + step] for step in range(2)]
    nodes = [jnp.concatenate([a.T, b.T], axis=1) for a, b in zip(own, sib)]
    pre = jnp.dot(jnp.concatenate(nodes), weights, preferred_element_type=F32)
    sigmoid = 0.5 * jnp.tanh(0.5 * pre) + 0.5
    slope = sigmoid * (1.0 + pre * (1.0 - sigmoid))
    cot = cot_ref[tile * TILE : (tile + 2) * TILE, :]
    grad = (cot.astype(F32) * slope).astype(BF16)
    wgrad = jnp.dot(jnp.concatenate(own, axis=1), grad, preferred_element_type=F32)
    mixed = lax.dot_general(
        weights[:TILE], grad, (((1,), (1,)), ((), ())), preferred_element_type=F32
    ).astype(BF16)
    return (pre * sigmoid).astype(BF16), wgrad, (mixed[:, :TILE], mixed[:, TILE:])


def ordered_weight(core_ref, weight_ref):
    core = core_ref[0]
    halves = [pl.ds(pl.multiple_of(at * TILE, TILE), TILE) for at in (core, 1 - core)]
    return jnp.concatenate([weight_ref[half, :] for half in halves])


def dense_kernel(core_ref, weight_ref, own_cot, sib_cot, own_sums, sib_sums, act_ref, *mixed_refs):
    weights = ordered_weight(core_ref, weight_ref)
    total = None
    for at in range(0, 16, 2):
        half, tile = divmod(at, 8)
        cot = sib_cot if half else own_cot
        act, wgrad, mixed = dense_pair(weights, half, tile, cot, own_sums, sib_sums)
        if not half:
            act_ref[tile * TILE : (tile + 2) * TILE, :] = act
        total = wgrad if total is None else total + wgrad
        for step, value in enumerate(mixed):
            third, place = third_of(at + step)
            mixed_refs[third][place] = value
    for part in range(EXTRA):
        extra = total[:, part * TILE : (part + 1) * TILE]
        mixed_refs[SIDE][CUTS[SIDE][1] - CUTS[SIDE][0] + part] = extra.astype(BF16)


def dense(core, weight, own_cot, sib_cot, own_sums, sib_sums):
    act, *mixed = pl.pallas_call(
        dense_kernel,
        out_shape=[jax.ShapeDtypeStruct(own_cot.shape, BF16)] + third_shapes(1, EXTRA),
        in_specs=[smem_spec()] + [vmem_spec()] * 5,
        out_specs=[vmem_spec()] * 4,
        compiler_params=pltpu.CompilerParams(vmem_limit_bytes=24 << 20),
        cost_estimate=cost(2 * 2048 * 256 * 512, 4 << 20),
        name="dense",
    )(core, weight, own_cot, sib_cot, own_sums, sib_sums)
    return act, mixed


def back_kernel(core_ref, own_ref, sib_ref, wgrad_ref, out_ref, weight_ref):
    core = core_ref[0]
    scale = 1.0 / math.sqrt(NODES)
    extra = sib_ref.shape[0] - EXTRA
    for ref, half in ((own_ref, core), (sib_ref, 1 - core)):
        lanes = pl.ds(pl.multiple_of(half * TILE, TILE), TILE)
        for tile in range(8):
            out_ref[tile * TILE : (tile + 1) * TILE, lanes] = ref[tile].T
    for ref, first, half in ((wgrad_ref, 0, core), (sib_ref, extra, 1 - core)):
        rows = pl.ds(pl.multiple_of(half * TILE, TILE), TILE)
        for part in range(EXTRA):
            lanes = slice(part * TILE, (part + 1) * TILE)
            weight_ref[rows, lanes] = ref[first + part].astype(F32) * scale


def turn_back(core, own_part, sib_part, wgrad):
    return pl.pallas_call(
        back_kernel,
        out_shape=[
            jax.ShapeDtypeStruct((8 * TILE, 2 * TILE), BF16),
            jax.ShapeDtypeStruct((2 * TILE, 2 * TILE), F32),
        ],
        in_specs=[smem_spec()] + [vmem_spec()] * 3,
        out_specs=[vmem_spec()] * 2,
        compiler_params=pltpu.CompilerParams(vmem_limit_bytes=8 << 20),
        cost_estimate=cost(0, 1 << 20),
        name="turn_back",
    )(core, own_part, sib_part, wgrad)


def body(features, weight, cotangent, blocks, block_row, block_col, counts):
    row_at, col_at = lax.axis_index("gr"), lax.axis_index("gc")
    y, xl, core = row_at // 4, (row_at // 2) % 2, row_at % 2
    xh, z = col_at // 4, col_at % 4
    core_arg = core.reshape(1).astype(jnp.int32)

    sib_feats = move(features, core=1)
    slices = turn_in(core_arg, features, sib_feats)

    own_tiles = blocks[0, 0]
    slots = own_tiles.shape[0]
    fetched = []

    def fetch(step, sent):
        if step == 2:
            event = sent[2]
            live = jnp.broadcast_to(after(counts[0, 0], event), (slots,))
            rows, cols = after(block_row[0, 0], event), after(block_col[0, 0], event)
            lists = jnp.stack([rows, cols, live])
            fetched.extend([lists, move(lists, core=1), move(after(cotangent, event), core=1)])

    gathered = spread(slices, GR_LINKS, fetch)
    own_lists, sib_lists, sib_cot = fetched
    sib_tiles = move(after(own_tiles, slices[0]), core=1)
    lists = jnp.stack([own_lists, sib_lists], axis=1)
    rows, cols, live = lists[0], lists[1], lists[2, :, 0]
    side = jnp.arange(2, dtype=jnp.int32)[:, None]
    part = rows // 8
    row_ids = (((part % 4) ^ z) * 2 + ((part // 4) ^ xh)) * 16 + side * 8 + rows % 8
    part = cols // 8
    col_ids = ((part // 4) ^ y) * 32 + (((part // 2) % 2) ^ xl) * 16
    col_ids = col_ids + ((part % 2) ^ core) * 8 + cols % 8
    dead = jnp.arange(slots, dtype=jnp.int32)[None, :] >= live[:, None]
    by_col = order_slots(col_ids, row_ids, dead)
    by_col = (after(by_col[0], sib_cot), by_col[1])
    by_row = order_slots(row_ids, col_ids, dead)

    parts, tiles = block_pass(False, live, by_col, (own_tiles, sib_tiles), gathered)
    own_sums = collect(parts, GC_LINKS)
    sib_sums = move(own_sums, core=1)

    activations, mixed = dense(core_arg, weight, cotangent, sib_cot, own_sums, sib_sums)

    gathered = spread(mixed, GC_LINKS, extra=EXTRA)
    parts, _ = block_pass(True, live, by_row, tiles, gathered)
    grads, wgrad = collect(parts, GR_LINKS, EXTRA)
    last = move(jnp.concatenate([grads[8:], wgrad]), core=1)
    feature_grad, weight_grad = turn_back(core_arg, grads[:8], last, wgrad)
    return (activations, weight_grad, feature_grad)


def solution(mesh):
    return jax.shard_map(
        body,
        mesh=mesh,
        in_specs=(
            P(("gr", "gc"), None),
            P(),
            P(("gr", "gc"), None),
            P("gr", "gc", None, None, None),
            P("gr", "gc", None),
            P("gr", "gc", None),
            P("gr", "gc"),
        ),
        out_specs=(P(("gr", "gc"), None), P(), P(("gr", "gc"), None)),
        check_vma=False,
    )
```
